256 devices in a mesh: half: 2 (over x_lo), panel: 4 (over x_hi, core), dom: 32 (over z, y).
Axes of the slice: x: 4 (x_hi: 2, x_lo: 2; x = x_hi * 2 + x_lo), y: 4, z: 8, core: 2. Of those that a mesh axis runs over, the one named last changes fastest.
Arguments:
- images: bfloat16 [4096, 8192], P(('half', 'dom')), parts along dimension 0, may hold values from -128 to 128
- shift_index: int32 [4096, 9], P(('half', 'dom')), parts along dimension 0, may hold values from 0 to 48, as said below
- references: bfloat16 [1024, 8192], P(('half', 'panel', 'dom')), parts along dimension 0, may hold values from -0.6 to 0.6
- slot_blocks: int32 [1024, 8], P(('half', 'panel')), parts along dimension 0, may hold values from 0 to 255
Outputs:
- volume: float32 [512, 1024], P(('half', 'panel', 'dom')), parts along dimension 0
- log_evidence: float32 [4096], P(('half', 'dom')), parts along dimension 0
The draws below stay inside these ranges and needn't reach their ends.
There are 2 independent parts, one for each index of `half`. The reference program is written for one: setup_inputs(seed, part) draws one part's arguments, and reference() takes and returns one part's arrays. A program takes and returns all parts, laid end to end along the dimension named above; each array names one. Nothing has to cross between parts.
Inputs may be any that keep to these rules, and one draw needn't show every extreme that they name: `shift_index`: each row names 9 different offsets.
All inputs are finite; a program needn't handle non-finite values.
Results may differ from the reference program's by a relative error of at most 0.0048.
Values may be sent and summed in bfloat16 or wider, within the bound.
No kernel may reach another device: no remote copies, remote signals or barrier semaphores. Data moves between devices by JAX's collectives and lax.ppermute only.
A program may use at most 128 MiB of HBM per device.

```python
import math
import jax
import jax.numpy as jnp
from jax import lax

PIX = 64
SHIFTS = 9
GRID = 7
SEG = 8
PARTICLES = 2048
ORIENT = 512
VB = 256
BLK = 1024


def ref_rows(key):
    key_base, key_scale = jax.random.split(key)
    row_width = 2 * PIX * PIX
    values = jnp.clip(jax.random.normal(key_base, (ORIENT, row_width), jnp.float32), -6.0, 6.0)
    row_scale = jnp.exp(jax.random.uniform(key_scale, (ORIENT,), jnp.float32, math.log(0.5), math.log(1.5)))
    return values * row_scale[:, None] / PIX


def shift_rows(key):
    offset_count = GRID * GRID
    noise = jax.random.randint(key, (PARTICLES, offset_count), 0, 1 << 20)
    ranking = noise * offset_count + jnp.arange(offset_count, dtype=jnp.int32)[None, :]
    _, chosen = lax.top_k(ranking, SHIFTS)
    return chosen.astype(jnp.int32)


def draw_references(key, part):
    return ref_rows(jax.random.fold_in(key, 101)).astype(jnp.bfloat16)


def draw_shift_index(key, part):
    return shift_rows(jax.random.fold_in(key, 202))


def draw_images(key, part):
    row_width = 2 * PIX * PIX
    key_base = jax.random.fold_in(jax.random.fold_in(key, 303), 0)
    return jnp.clip(jax.random.normal(key_base, (PARTICLES, row_width), jnp.float32), -6.0, 6.0).astype(jnp.bfloat16)


def place_ends(drawn, stream_key, least, largest):
    dims = drawn.shape
    spot = [jax.random.randint(jax.random.fold_in(stream_key, axis), (), 0, dims[axis]) for axis in range(len(dims))]
    drawn = drawn.at[tuple(spot)].set(least)
    longest = dims.index(max(dims))
    spot[longest] = (spot[longest] + 1) % dims[longest]
    return drawn.at[tuple(spot)].set(largest)


def setup_inputs(seed: int = 0, part: int = 0) -> dict:
    key_list = jax.random.split(jax.random.key(seed), 5)
    part_splits = jax.random.split(jax.random.fold_in(key_list[4], part), 5)
    images = draw_images(jax.random.fold_in(jax.random.fold_in(key_list[4], part), 71), part)
    shift_index = draw_shift_index(jax.random.fold_in(jax.random.fold_in(key_list[4], part), 71), part)
    references = draw_references(jax.random.fold_in(jax.random.fold_in(key_list[4], part), 71), part)
    slot_blocks = place_ends(jax.random.randint(part_splits[3], (ORIENT, SEG), 0, VB), jax.random.fold_in(part_splits[3], 1), 0, VB - 1).astype(jnp.int32)
    return dict(images=images, shift_index=shift_index, references=references, slot_blocks=slot_blocks)


offset_sigma = 2.0


def offsets(shift_index):
    shift_row = (shift_index // GRID - GRID // 2).astype(jnp.float32)
    shift_col = (shift_index % GRID - GRID // 2).astype(jnp.float32)
    return shift_row, shift_col


def penalty(shift_index):
    shift_row, shift_col = offsets(shift_index)
    return (shift_row * shift_row + shift_col * shift_col) * (0.5 / (offset_sigma * offset_sigma))


def phase_table():
    shift_row, shift_col = offsets(jnp.arange(GRID * GRID, dtype=jnp.int32))
    frequency = jnp.arange(PIX, dtype=jnp.float32) - PIX // 2
    phase_angle = (-2.0 * math.pi / PIX) * (shift_row[:, None, None] * frequency[None, :, None] + shift_col[:, None, None] * frequency[None, None, :])
    return jnp.cos(phase_angle), jnp.sin(phase_angle)


def shift_images(images, shift_index, cos_table, sin_table):
    row_count = images.shape[0]
    cosine = cos_table[shift_index]
    sine_part = sin_table[shift_index]
    picture = images.astype(jnp.float32).reshape(row_count, 1, PIX, 2, PIX)
    real_part = picture[:, :, :, 0, :]
    imag_part = picture[:, :, :, 1, :]
    out_real = real_part * cosine - imag_part * sine_part
    out_imag = real_part * sine_part + imag_part * cosine
    return jnp.stack([out_real, out_imag], axis=3).reshape(row_count * SHIFTS, 2 * PIX * PIX).astype(jnp.bfloat16)


def reference(images, shift_index, references, slot_blocks):
    cos_table, sin_table = phase_table()
    block_size = math.gcd(PARTICLES, 64)
    block_count = PARTICLES // block_size
    ref_norms = jnp.sum(jnp.square(references.astype(jnp.float32)), axis=1)
    image_blocks = images.reshape(block_count, block_size, 2 * PIX * PIX)
    index_blocks = shift_index.reshape(block_count, block_size, SHIFTS)

    def one_block(blocks):
        image_block, index_block = blocks
        moved = shift_images(image_block, index_block, cos_table, sin_table)
        correlation = lax.dot_general(moved, references, (((1,), (1,)), ((), ())), preferred_element_type=jnp.float32)
        return correlation - 0.5 * ref_norms[None, :] - penalty(index_block).reshape(-1, 1)

    scores = lax.map(one_block, (image_blocks, index_blocks)).reshape(PARTICLES, SHIFTS * ORIENT)
    row_top = jnp.max(scores, axis=1)
    raised = jnp.exp(scores - row_top[:, None])
    row_total = jnp.sum(raised, axis=1)
    weights = (raised / row_total[:, None]).astype(jnp.bfloat16)
    log_evidence = row_top + jnp.log(row_total)
    weight_blocks = weights.reshape(block_count, block_size * SHIFTS, ORIENT)

    def add_block(running, inputs):
        image_block, index_block, weight_block = inputs
        moved = shift_images(image_block, index_block, cos_table, sin_table)
        return running + lax.dot_general(weight_block, moved, (((0,), (0,)), ((), ())), preferred_element_type=jnp.float32), None

    slab_sums, _ = lax.scan(add_block, jnp.zeros((ORIENT, 2 * PIX * PIX), jnp.float32), (image_blocks, index_blocks, weight_blocks))
    summed = jnp.zeros((VB, BLK), jnp.float32).at[slot_blocks.reshape(-1)].add(slab_sums.reshape(ORIENT * SEG, BLK))
    return summed * (PARTICLES * SEG / VB) ** -0.5, log_evidence
```

```python
import functools
import math

import jax
import jax.numpy as jnp
import numpy as np
from jax import lax
from jax.experimental import pallas as pl
from jax.experimental.pallas import tpu as pltpu
from jax.sharding import Mesh
from jax.sharding import PartitionSpec as P

PIX = 64
SHIFTS = 9
GRID = 7
OFFS = GRID * GRID
KPAD = 160
Z, Y = 8, 4
SEG = 8
BLK = 1024
VB = 256
OFFSET_SIGMA = 2.0
BF16 = jnp.bfloat16
F32 = jnp.float32


def dom_of(z, y):
    return (z % Z) * Y + y % Y


COSETS = [[dom_of((c - 2 * (j // 2)) % 4 + 4 * (j % 2), j // 2) for j in range(8)] for c in range(4)]


def receive_from(dz, dy):
    return [(dom_of(z + dz, y + dy), dom_of(z, y)) for z in range(Z) for y in range(Y)]


def phase_parts():
    offset = np.arange(OFFS)
    a, b = offset // GRID - GRID // 2, offset % GRID - GRID // 2
    f = np.arange(PIX) - PIX // 2
    turns = (f[:, None, None] * a[None, :, None] + f[None, None, :] * b[None, :, None]) % PIX
    angle = -2.0 * math.pi / PIX * turns
    cos, sin = np.cos(angle), np.sin(angle)
    table = np.concatenate([cos, cos, -sin, sin], axis=2).astype(np.float32)
    high = table.astype(BF16)
    rest = table - high.astype(np.float32)
    mid = rest.astype(BF16)
    low = (rest - mid.astype(np.float32)).astype(BF16)
    pad = np.zeros((PIX, KPAD - 3 * OFFS, 4 * PIX), BF16)
    return np.concatenate([high, mid, low, pad], axis=1)


def shift_kernel(index_ref, image_ref, table_ref, out_ref, pen_ref, hot_ref):
    rows = image_ref.shape[0]

    @pl.when(pl.program_id(0) == 0)
    def _():
        k = lax.broadcasted_iota(jnp.int32, (KPAD, rows), 0)
        offset = jnp.where(k < 3 * OFFS, k % OFFS, -1)
        hot_t = jnp.concatenate(
            [jnp.where(offset == index_ref[t : t + 1, :], 1.0, 0.0) for t in range(SHIFTS)], axis=1
        )
        hot_ref[...] = hot_t.T.astype(BF16)
        k = lax.broadcasted_iota(jnp.int32, (8, KPAD), 1)
        a, b = k // GRID - GRID // 2, k % GRID - GRID // 2
        cost = (a * a + b * b).astype(F32) * (0.5 / (OFFSET_SIGMA * OFFSET_SIGMA))
        pen_ref[...] = jnp.dot(
            jnp.where(k < OFFS, cost, 0.0).astype(BF16), hot_t.astype(BF16), preferred_element_type=F32
        )

    for u in range(table_ref.shape[0]):
        phase = jnp.dot(hot_ref[...], table_ref[u], preferred_element_type=F32)
        cols = slice(u * 2 * PIX, (u + 1) * 2 * PIX)
        x = image_ref[:, cols].astype(F32)
        swapped = pltpu.roll(x, PIX, 1)
        for t in range(SHIFTS):
            part = phase[t * rows : (t + 1) * rows]
            out_ref[t * rows : (t + 1) * rows, cols] = (
                x * part[:, : 2 * PIX] + swapped * part[:, 2 * PIX :]
            ).astype(BF16)


def shift_images(images, index_t, table):
    rows, width = images.shape
    steps = 8
    total = rows * SHIFTS
    return pl.pallas_call(
        shift_kernel,
        grid=(steps,),
        in_specs=[
            pl.BlockSpec((SHIFTS, rows), lambda s: (0, 0)),
            pl.BlockSpec((rows, width // steps), lambda s: (0, s)),
            pl.BlockSpec((PIX // steps, KPAD, 4 * PIX), lambda s: (s, 0, 0)),
        ],
        out_specs=[
            pl.BlockSpec((total, width // steps), lambda s: (0, s)),
            pl.BlockSpec((8, total), lambda s: (0, 0)),
        ],
        out_shape=[
            jax.ShapeDtypeStruct((total, width), BF16),
            jax.ShapeDtypeStruct((8, total), F32),
        ],
        scratch_shapes=[pltpu.VMEM((total, KPAD), BF16)],
        compiler_params=pltpu.CompilerParams(vmem_limit_bytes=24 << 20),
        cost_estimate=pl.CostEstimate(flops=5 * 10**9, bytes_accessed=16 << 20, transcendentals=0),
        name="shift",
    )(index_t, images, table)


def tile_shifts(x):
    return jnp.concatenate([x] * SHIFTS, axis=1)


def over_shifts(op, x, rows):
    return functools.reduce(op, [x[:, t * rows : (t + 1) * rows] for t in range(SHIFTS)])


def score_kernel(own, up, down, right, left, moved, pen, raised, stats, acc, norm):
    step = pl.program_id(0)
    refs = jnp.concatenate([own[...], up[...], down[...], right[...], left[...]], axis=0)
    part = lax.dot_general(refs, moved[...], (((1,), (1,)), ((), ())), preferred_element_type=F32)
    wide = refs.astype(F32)
    square = jnp.sum(wide * wide, axis=1, keepdims=True)

    @pl.when(step == 0)
    def _():
        acc[...] = part
        norm[...] = square

    @pl.when(step > 0)
    def _():
        acc[...] += part
        norm[...] += square

    @pl.when(step == pl.num_programs(0) - 1)
    def _():
        rows = acc.shape[1] // SHIFTS
        scores = acc[...] - 0.5 * norm[...] - pen[0:1, :]
        top = over_shifts(jnp.maximum, jnp.max(scores, axis=0, keepdims=True), rows)
        value = jnp.exp(scores - tile_shifts(top))
        raised[...] = value
        total = over_shifts(jnp.add, jnp.sum(value, axis=0, keepdims=True), rows)
        stats[...] = jnp.concatenate([top, total], axis=0)


def score(pieces, moved, pen):
    total, width = moved.shape
    steps = 8
    count = sum(p.shape[0] for p in pieces)
    return pl.pallas_call(
        score_kernel,
        grid=(steps,),
        in_specs=[pl.BlockSpec((p.shape[0], width // steps), lambda s: (0, s)) for p in pieces]
        + [
            pl.BlockSpec((total, width // steps), lambda s: (0, s)),
            pl.BlockSpec((8, total), lambda s: (0, 0)),
        ],
        out_specs=[
            pl.BlockSpec((count, total), lambda s: (0, 0)),
            pl.BlockSpec((2, total // SHIFTS), lambda s: (0, 0)),
        ],
        out_shape=[
            jax.ShapeDtypeStruct((count, total), F32),
            jax.ShapeDtypeStruct((2, total // SHIFTS), F32),
        ],
        scratch_shapes=[pltpu.VMEM((count, total), F32), pltpu.VMEM((count, 1), F32)],
        compiler_params=pltpu.CompilerParams(vmem_limit_bytes=24 << 20),
        cost_estimate=pl.CostEstimate(flops=2 * 10**9, bytes_accessed=12 << 20, transcendentals=1 << 17),
        name="score",
    )(*pieces, moved, pen)


def insert_kernel(scale, raised, s0, s1, s2, s3, slot_ref, moved, mine, other, evidence, acc, weight, slots):
    step = pl.program_id(0)
    count = raised.shape[0]

    @pl.when(step == 0)
    def _():
        tops = [s[0:1, :] for s in (s0, s1, s2, s3)]
        sums = [s[1:2, :] for s in (s0, s1, s2, s3)]
        top = functools.reduce(jnp.maximum, tops)
        total = functools.reduce(jnp.add, [b * jnp.exp(a - top) for a, b in zip(tops, sums)])
        evidence[...] = top + jnp.log(total)
        factor = jnp.exp(tops[0] - top) / total
        weight[...] = (raised[...] * tile_shifts(factor)).astype(BF16)
        dom = lax.axis_index("dom")
        coset = (dom // Y + 2 * (dom % Y)) % 4
        q = lax.broadcasted_iota(jnp.int32, (count, count), 1) // 4
        group = q // 8
        j = q % 8
        ahead = jnp.where(group == 1, 1, jnp.where(group == 2, 3, jnp.where(group == 3, 2, 0)))
        c = (coset + ahead) % 4
        y = j // 2
        z = (c + 4 - 2 * (y % 2)) % 4 + 4 * (j % 2)
        source = (z * Y + y) * 4 + lax.broadcasted_iota(jnp.int32, (count, count), 1) % 4
        order = jnp.where(lax.broadcasted_iota(jnp.int32, (count, count), 0) == source, 1.0, 0.0)
        slots[...] = jnp.dot(
            slot_ref[...].astype(F32).astype(BF16), order.astype(BF16), preferred_element_type=F32
        ).astype(jnp.int32)

    core = lax.axis_index("core")
    m = lax.broadcasted_iota(jnp.int32, (VB, count), 0)
    half = m % (VB // 2)
    owner = jnp.where(m < VB // 2, core, 1 - core)
    block = half // (VB // 4) * (VB // 2) + owner * (VB // 4) + half % (VB // 4)
    hot = jnp.where(block == slots[pl.ds(step, 1), :], 1.0, 0.0).astype(BF16)
    blocked = jnp.dot(hot, weight[...], preferred_element_type=F32).astype(BF16)
    part = jnp.dot(blocked, moved[...], preferred_element_type=F32)

    @pl.when(step == 0)
    def _():
        acc[...] = part

    @pl.when(step > 0)
    def _():
        acc[...] += part

    @pl.when(step == pl.num_programs(0) - 1)
    def _():
        mine[...] = acc[: VB // 2] * scale
        other[...] = (acc[VB // 2 :] * scale).astype(BF16)


def insert(raised, stats, slots_t, moved, scale):
    count, total = raised.shape
    rows = total // SHIFTS
    return pl.pallas_call(
        functools.partial(insert_kernel, scale),
        grid=(SEG,),
        in_specs=[pl.BlockSpec((count, total), lambda s: (0, 0))]
        + [pl.BlockSpec((2, rows), lambda s: (0, 0))] * 4
        + [
            pl.BlockSpec((SEG, count), lambda s: (0, 0)),
            pl.BlockSpec((total, BLK), lambda s: (0, s)),
        ],
        out_specs=[
            pl.BlockSpec((VB // 2, BLK), lambda s: (0, 0)),
            pl.BlockSpec((VB // 2, BLK), lambda s: (0, 0)),
            pl.BlockSpec((1, rows), lambda s: (0, 0)),
        ],
        out_shape=[
            jax.ShapeDtypeStruct((VB // 2, BLK), F32),
            jax.ShapeDtypeStruct((VB // 2, BLK), BF16),
            jax.ShapeDtypeStruct((1, rows), F32),
        ],
        scratch_shapes=[
            pltpu.VMEM((VB, BLK), F32),
            pltpu.VMEM((count, total), BF16),
            pltpu.VMEM((SEG, count), jnp.int32),
        ],
        compiler_params=pltpu.CompilerParams(vmem_limit_bytes=24 << 20),
        cost_estimate=pl.CostEstimate(flops=3 * 10**9, bytes_accessed=12 << 20, transcendentals=0),
        name="insert",
    )(raised, *stats, slots_t, moved)


def shards(images, shift_index, references, slot_blocks):
    rows = images.shape[0]
    scale = (rows * Z * Y * SEG / VB) ** (-0.5)
    copies = jnp.broadcast_to(references[None], (8, *references.shape))
    own = lax.all_to_all(copies, "dom", 0, 0, axis_index_groups=COSETS, tiled=True)
    own = own.reshape(8 * references.shape[0], references.shape[1])
    near = own.shape[0] // 2
    up = lax.ppermute(own, "dom", receive_from(1, 0))
    down = lax.ppermute(own, "dom", receive_from(-1, 0))
    right = lax.ppermute(own[:near], "dom", receive_from(0, 1))
    left = lax.ppermute(own[near:], "dom", receive_from(0, -1))
    moved, pen = shift_images(images, shift_index.T, jnp.asarray(phase_parts()))
    raised, stats = score((own, up, down, right, left), moved, pen)
    swap = [(0, 1), (1, 0)]
    everyone = [
        stats,
        lax.ppermute(stats, "core", swap),
        lax.ppermute(stats, "px", swap),
        lax.ppermute(stats, ("px", "core"), [(i, 3 - i) for i in range(4)]),
    ]
    mine, other, evidence = insert(raised, everyone, slot_blocks.T, moved, scale)
    paired = mine + lax.ppermute(other, "core", swap).astype(F32)
    sent = paired.astype(BF16).reshape(2 * Z * Y, VB // (4 * Z * Y), BLK)
    arrived = lax.all_to_all(sent, ("px", "dom"), 0, 0, tiled=True)
    return (jnp.sum(arrived.astype(F32), axis=0), evidence.reshape(rows))


def solution(mesh):
    split = Mesh(mesh.devices.reshape(2, 2, 2, Z * Y), ("half", "px", "core", "dom"))
    in_specs = (
        P(("half", "dom"), None),
        P(("half", "dom"), None),
        P(("half", "px", "core", "dom"), None),
        P(("half", "px", "core"), None),
    )
    out_specs = (P(("half", "px", "core", "dom"), None), P(("half", "dom")))
    return jax.shard_map(shards, mesh=split, in_specs=in_specs, out_specs=out_specs, check_vma=False)
```

```python
import functools
import math

import jax
import jax.numpy as jnp
import numpy as np
from jax import lax
from jax.experimental import pallas as pl
from jax.experimental.pallas import tpu as pltpu
from jax.sharding import Mesh
from jax.sharding import PartitionSpec as P

PIX = 64
SHIFTS = 9
GRID = 7
OFFS = GRID * GRID
KPAD = 112
Z, Y = 8, 4
SEG = 8
BLK = 1024
VB = 256
OFFSET_SIGMA = 2.0
BF16 = jnp.bfloat16
F32 = jnp.float32


def dom_of(z, y):
    return (z % Z) * Y + y % Y


FAR = ((0, 0), (4, 0), (2, 2), (-2, 2))
NEAR = ((0, 0), (1, 0), (-1, 0), (0, 1), (0, -1), (1, 1), (-1, 1), (0, 2))


def receive_from(dz, dy):
    return [(dom_of(z + dz, y + dy), dom_of(z, y)) for z in range(Z) for y in range(Y)]


def phase_parts():
    offset = np.arange(OFFS)
    a, b = offset // GRID - GRID // 2, offset % GRID - GRID // 2
    f = np.arange(PIX) - PIX // 2
    turns = (f[:, None, None] * a[None, :, None] + f[None, None, :] * b[None, :, None]) % PIX
    angle = -2.0 * math.pi / PIX * turns
    cos, sin = np.cos(angle), np.sin(angle)
    table = np.concatenate([cos, cos, -sin, sin], axis=2).astype(np.float32)
    high = table.astype(BF16)
    low = (table - high.astype(np.float32)).astype(BF16)
    pad = np.zeros((PIX, KPAD - 2 * OFFS, 4 * PIX), BF16)
    return np.concatenate([high, low, pad], axis=1)


def one_hot(index_ref):
    rows = index_ref.shape[1]
    k = lax.broadcasted_iota(jnp.int32, (KPAD, rows), 0)
    offset = jnp.where(k < 2 * OFFS, k % OFFS, -1)
    return jnp.concatenate(
        [jnp.where(offset == index_ref[t : t + 1, :], 1.0, 0.0) for t in range(SHIFTS)], axis=1
    )


def shift_kernel(start, index_ref, image_ref, table_ref, out_ref, hot_ref):
    rows = image_ref.shape[0]
    hot_ref[...] = one_hot(index_ref).T.astype(BF16)
    for u in range(table_ref.shape[0]):
        phase = jnp.dot(hot_ref[...], table_ref[u], preferred_element_type=F32)
        cols = slice(u * 2 * PIX, (u + 1) * 2 * PIX)
        source = slice((start + u) * 2 * PIX, (start + u + 1) * 2 * PIX)
        x = image_ref[:, source].astype(F32)
        swapped = pltpu.roll(x, PIX, 1)
        for t in range(SHIFTS):
            part = phase[t * rows : (t + 1) * rows]
            out_ref[t * rows : (t + 1) * rows, cols] = (
                x * part[:, : 2 * PIX] + swapped * part[:, 2 * PIX :]
            ).astype(BF16)


VMEM = pl.BlockSpec(memory_space=pltpu.VMEM)


def params():
    return pltpu.CompilerParams(vmem_limit_bytes=24 << 20)


def shift_images(images, index_t, table, start):
    total = images.shape[0] * SHIFTS
    count = table.shape[0]
    return pl.pallas_call(
        functools.partial(shift_kernel, start),
        in_specs=[VMEM] * 3,
        out_specs=VMEM,
        out_shape=jax.ShapeDtypeStruct((total, count * 2 * PIX), BF16),
        scratch_shapes=[pltpu.VMEM((total, KPAD), BF16)],
        compiler_params=params(),
        cost_estimate=pl.CostEstimate(flops=count * 10**8, bytes_accessed=count << 18, transcendentals=0),
        name="shift",
    )(index_t, images, jnp.asarray(table))


def choose(g, values):
    out = jnp.zeros_like(g)
    for i, v in enumerate(values):
        if v:
            out = jnp.where(g == i, v, out)
    return out


def slots_kernel(slot_ref, hot_ref):
    count = slot_ref.shape[1]
    dom = lax.axis_index("dom")
    q = lax.broadcasted_iota(jnp.int32, (count, count), 1)
    piece, j = q // 16, (q // 4) % 4
    z = (dom // Y + choose(piece, [d for d, _ in NEAR]) + choose(j, [d for d, _ in FAR]) + Z) % Z
    y = (dom % Y + choose(piece, [d for _, d in NEAR]) + choose(j, [d for _, d in FAR]) + Y) % Y
    source = (z * Y + y) * 4 + q % 4
    order = jnp.where(lax.broadcasted_iota(jnp.int32, (count, count), 0) == source, 1.0, 0.0)
    slots = jnp.dot(
        slot_ref[...].astype(F32).astype(BF16), order.astype(BF16), preferred_element_type=F32
    ).astype(jnp.int32)
    core = lax.axis_index("core")
    m = lax.broadcasted_iota(jnp.int32, (VB, count), 0)
    half = m % (VB // 2)
    owner = jnp.where(m < VB // 2, core, 1 - core)
    block = half // (VB // 4) * (VB // 2) + owner * (VB // 4) + half % (VB // 4)
    for s in range(SEG):
        hot_ref[s] = jnp.where(block == slots[s : s + 1, :], 1.0, 0.0).astype(BF16)


def place_slots(slots_t):
    return pl.pallas_call(
        slots_kernel,
        in_specs=[VMEM],
        out_specs=VMEM,
        out_shape=jax.ShapeDtypeStruct((SEG, VB, slots_t.shape[1]), BF16),
        compiler_params=params(),
        cost_estimate=pl.CostEstimate(flops=10**8, bytes_accessed=4 << 20, transcendentals=0),
        name="slots",
    )(slots_t)


def tile_shifts(x):
    return jnp.concatenate([x] * SHIFTS, axis=1)


def over_shifts(op, x, rows):
    return functools.reduce(op, [x[:, t * rows : (t + 1) * rows] for t in range(SHIFTS)])


def score_kernel(n_moved, *refs):
    index_ref, raised, stats, acc = refs[-4:]
    moved, pieces = refs[:n_moved], refs[n_moved:-4]
    count, total = acc.shape
    acc[...] = jnp.zeros_like(acc)
    norm = jnp.zeros((count, 1), F32)
    start = 0
    for m in moved:
        for c in range(m.shape[1] // BLK):
            at = slice(start + c * BLK, start + (c + 1) * BLK)
            some = jnp.concatenate([p[:, at] for p in pieces], axis=0)
            acc[...] += lax.dot_general(
                some, m[:, c * BLK : (c + 1) * BLK], (((1,), (1,)), ((), ())), preferred_element_type=F32
            )
            wide = some.astype(F32)
            norm += jnp.sum(wide * wide, axis=1, keepdims=True)
        start += m.shape[1]
    k = lax.broadcasted_iota(jnp.int32, (8, KPAD), 1)
    a, b = k // GRID - GRID // 2, k % GRID - GRID // 2
    cost = (a * a + b * b).astype(F32) * (0.5 / (OFFSET_SIGMA * OFFSET_SIGMA))
    pen = jnp.dot(
        jnp.where(k < OFFS, cost, 0.0).astype(BF16), one_hot(index_ref).astype(BF16), preferred_element_type=F32
    )
    rows = total // SHIFTS
    scores = acc[...] - 0.5 * norm - pen[0:1, :]
    top = over_shifts(jnp.maximum, jnp.max(scores, axis=0, keepdims=True), rows)
    value = jnp.exp(scores - tile_shifts(top))
    raised[...] = value
    stats[0:1, :] = top
    stats[1:2, :] = over_shifts(jnp.add, jnp.sum(value, axis=0, keepdims=True), rows)


def score(pieces, moved, index_t):
    total = moved[0].shape[0]
    count = sum(p.shape[0] for p in pieces)
    return pl.pallas_call(
        functools.partial(score_kernel, len(moved)),
        in_specs=[VMEM] * (len(pieces) + len(moved) + 1),
        out_specs=[VMEM, VMEM],
        out_shape=[
            jax.ShapeDtypeStruct((count, total), F32),
            jax.ShapeDtypeStruct((2, total // SHIFTS), F32),
        ],
        scratch_shapes=[pltpu.VMEM((count, total), F32)],
        compiler_params=params(),
        cost_estimate=pl.CostEstimate(flops=2 * 10**9, bytes_accessed=12 << 20, transcendentals=1 << 17),
        name="score",
    )(*moved, *pieces, index_t)


def insert_kernel(scale, raised, s0, s1, s2, s3, hot, *rest):
    moved, (mine, other, evidence, acc, weight) = rest[:-5], rest[-5:]
    tops = [s[0:1, :] for s in (s0, s1, s2, s3)]
    sums = [s[1:2, :] for s in (s0, s1, s2, s3)]
    top = functools.reduce(jnp.maximum, tops)
    total = functools.reduce(jnp.add, [b * jnp.exp(a - top) for a, b in zip(tops, sums)])
    evidence[...] = top + jnp.log(total)
    factor = jnp.exp(tops[0] - top) / total
    weight[...] = (raised[...] * tile_shifts(factor)).astype(BF16)
    acc[...] = jnp.zeros_like(acc)

    start = 0
    for part in moved:
        for s in range(part.shape[1] // BLK):
            blocked = jnp.dot(hot[start + s], weight[...], preferred_element_type=F32).astype(BF16)
            acc[...] += jnp.dot(blocked, part[:, s * BLK : (s + 1) * BLK], preferred_element_type=F32)
        start += part.shape[1] // BLK
    mine[...] = acc[: VB // 2] * scale
    other[...] = (acc[VB // 2 :] * scale).astype(BF16)


def insert(raised, stats, hot, moved, scale):
    count, total = raised.shape
    rows = total // SHIFTS
    return pl.pallas_call(
        functools.partial(insert_kernel, scale),
        in_specs=[VMEM] * (6 + len(moved)),
        out_specs=[VMEM] * 3,
        out_shape=[
            jax.ShapeDtypeStruct((VB // 2, BLK), F32),
            jax.ShapeDtypeStruct((VB // 2, BLK), BF16),
            jax.ShapeDtypeStruct((1, rows), F32),
        ],
        scratch_shapes=[pltpu.VMEM((VB, BLK), F32), pltpu.VMEM((count, total), BF16)],
        compiler_params=params(),
        cost_estimate=pl.CostEstimate(flops=3 * 10**9, bytes_accessed=12 << 20, transcendentals=0),
        name="insert",
    )(raised, *stats, hot, *moved)


def gather(references, work):
    far = [lax.ppermute(references, "dom", receive_from(*d)) for d in FAR[1:]]
    far, done = lax.optimization_barrier((far, work[0]()))
    results = [done]
    own = jnp.concatenate([references, *far], axis=0)
    first = [lax.ppermute(own, "dom", receive_from(*d)) for d in NEAR[1:5]]
    up, done = lax.optimization_barrier((first[2], work[1]()))
    results.append(done)
    second = [lax.ppermute(up, "dom", receive_from(*d)) for d in ((1, 0), (-1, 0), (0, 1))]
    results.append(work[2]())
    return [own, *first, *second], results


def shards(images, shift_index, references, slot_blocks):
    rows = images.shape[0]
    scale = (rows * Z * Y * SEG / VB) ** (-0.5)
    index_t, table = shift_index.T, phase_parts()
    cuts = (0, 24, 40, 64)
    pieces, moved = gather(
        references,
        [functools.partial(shift_images, images, index_t, table[a:b], a) for a, b in zip(cuts, cuts[1:])],
    )
    hot = place_slots(slot_blocks.T)
    raised, stats = score(pieces, moved, index_t)
    swap = [(0, 1), (1, 0)]
    everyone = [
        stats,
        lax.ppermute(stats, "core", swap),
        lax.ppermute(stats, "px", swap),
        lax.ppermute(stats, ("px", "core"), [(i, 3 - i) for i in range(4)]),
    ]
    mine, other, evidence = insert(raised, everyone, hot, moved, scale)
    paired = mine + lax.ppermute(other, "core", swap).astype(F32)
    sent = paired.astype(BF16).reshape(2 * Z * Y, VB // (4 * Z * Y), BLK)
    arrived = lax.all_to_all(sent, ("px", "dom"), 0, 0, tiled=True)
    return (jnp.sum(arrived.astype(F32), axis=0), evidence.reshape(rows))


def solution(mesh):
    split = Mesh(mesh.devices.reshape(2, 2, 2, Z * Y), ("half", "px", "core", "dom"))
    in_specs = (
        P(("half", "dom"), None),
        P(("half", "dom"), None),
        P(("half", "px", "core", "dom"), None),
        P(("half", "px", "core"), None),
    )
    out_specs = (P(("half", "px", "core", "dom"), None), P(("half", "dom")))
    return jax.shard_map(shards, mesh=split, in_specs=in_specs, out_specs=out_specs, check_vma=False)
```

```python
import functools
import math

import jax
import jax.numpy as jnp
import numpy as np
from jax import lax
from jax.experimental import pallas as pl
from jax.experimental.pallas import tpu as pltpu
from jax.sharding import Mesh
from jax.sharding import PartitionSpec as P

PIX = 64
SHIFTS = 9
GRID = 7
OFFS = GRID * GRID
KPAD = 112
CUT = 24
Z, Y = 8, 4
SEG = 8
BLK = 1024
VB = 256
OFFSET_SIGMA = 2.0
BF16 = jnp.bfloat16
F32 = jnp.float32


def dom_of(z, y):
    return (z % Z) * Y + y % Y


FAR = ((0, 0), (4, 0), (2, 2), (-2, 2))
NEAR = ((0, 0), (1, 0), (-1, 0), (0, 1), (0, -1), (1, 1), (-1, 1), (0, 2))


def receive_from(dz, dy):
    return [(dom_of(z + dz, y + dy), dom_of(z, y)) for z in range(Z) for y in range(Y)]


def phase_parts():
    offset = np.arange(OFFS)
    a, b = offset // GRID - GRID // 2, offset % GRID - GRID // 2
    f = np.arange(PIX) - PIX // 2
    turns = (f[:, None, None] * a[None, :, None] + f[None, None, :] * b[None, :, None]) % PIX
    angle = -2.0 * math.pi / PIX * turns
    cos, sin = np.cos(angle), np.sin(angle)
    table = np.concatenate([cos, cos, -sin, sin], axis=2).astype(np.float32)
    high = table.astype(BF16)
    low = (table - high.astype(np.float32)).astype(BF16)
    pad = np.zeros((PIX, KPAD - 2 * OFFS, 4 * PIX), BF16)
    return np.concatenate([high, low, pad], axis=1)


def one_hot(index_ref):
    rows = index_ref.shape[1]
    k = lax.broadcasted_iota(jnp.int32, (KPAD, rows), 0)
    offset = jnp.where(k < 2 * OFFS, k % OFFS, -1)
    return jnp.concatenate(
        [jnp.where(offset == index_ref[t : t + 1, :], 1.0, 0.0) for t in range(SHIFTS)], axis=1
    )


def shift_kernel(start, index_ref, image_ref, table_ref, out_ref, hot_ref):
    rows = image_ref.shape[0]
    hot_ref[...] = one_hot(index_ref).T.astype(BF16)
    for u in range(table_ref.shape[0]):
        phase = jnp.dot(hot_ref[...], table_ref[u], preferred_element_type=F32)
        cols = slice(u * 2 * PIX, (u + 1) * 2 * PIX)
        source = slice((start + u) * 2 * PIX, (start + u + 1) * 2 * PIX)
        x = image_ref[:, source].astype(F32)
        swapped = pltpu.roll(x, PIX, 1)
        for t in range(SHIFTS):
            part = phase[t * rows : (t + 1) * rows]
            out_ref[t * rows : (t + 1) * rows, cols] = (
                x * part[:, : 2 * PIX] + swapped * part[:, 2 * PIX :]
            ).astype(BF16)


VMEM = pl.BlockSpec(memory_space=pltpu.VMEM)


def params():
    return pltpu.CompilerParams(vmem_limit_bytes=24 << 20)


def shift_images(images, index_t, table, start):
    total = images.shape[0] * SHIFTS
    count = table.shape[0]
    return pl.pallas_call(
        functools.partial(shift_kernel, start),
        in_specs=[VMEM] * 3,
        out_specs=VMEM,
        out_shape=jax.ShapeDtypeStruct((total, count * 2 * PIX), BF16),
        scratch_shapes=[pltpu.VMEM((total, KPAD), BF16)],
        compiler_params=params(),
        cost_estimate=pl.CostEstimate(flops=count * 10**8, bytes_accessed=count << 18, transcendentals=0),
        name="shift",
    )(index_t, images, jnp.asarray(table))


def choose(g, values):
    out = jnp.zeros_like(g)
    for i, v in enumerate(values):
        if v:
            out = jnp.where(g == i, v, out)
    return out


def slots_kernel(slot_ref, hot_ref):
    count = slot_ref.shape[1]
    dom = lax.axis_index("dom")
    q = lax.broadcasted_iota(jnp.int32, (count, count), 1)
    piece, j = q // 16, (q // 4) % 4
    z = (dom // Y + choose(piece, [d for d, _ in NEAR]) + choose(j, [d for d, _ in FAR]) + Z) % Z
    y = (dom % Y + choose(piece, [d for _, d in NEAR]) + choose(j, [d for _, d in FAR]) + Y) % Y
    source = (z * Y + y) * 4 + q % 4
    order = jnp.where(lax.broadcasted_iota(jnp.int32, (count, count), 0) == source, 1.0, 0.0)
    slots = jnp.dot(
        slot_ref[...].astype(F32).astype(BF16), order.astype(BF16), preferred_element_type=F32
    ).astype(jnp.int32)
    core = lax.axis_index("core")
    m = lax.broadcasted_iota(jnp.int32, (VB, count), 0)
    half = m % (VB // 2)
    owner = jnp.where(m < VB // 2, core, 1 - core)
    block = half // (VB // 4) * (VB // 2) + owner * (VB // 4) + half % (VB // 4)
    for s in range(SEG):
        hot_ref[s] = jnp.where(block == slots[s : s + 1, :], 1.0, 0.0).astype(BF16)


def place_slots(slots_t):
    return pl.pallas_call(
        slots_kernel,
        in_specs=[VMEM],
        out_specs=VMEM,
        out_shape=jax.ShapeDtypeStruct((SEG, VB, slots_t.shape[1]), BF16),
        compiler_params=params(),
        cost_estimate=pl.CostEstimate(flops=10**8, bytes_accessed=4 << 20, transcendentals=0),
        name="slots",
    )(slots_t)


def tile_shifts(x):
    return jnp.concatenate([x] * SHIFTS, axis=1)


def over_shifts(op, x, rows):
    return functools.reduce(op, [x[:, t * rows : (t + 1) * rows] for t in range(SHIFTS)])


def score_kernel(n_moved, *refs):
    index_ref, raised, stats, acc = refs[-4:]
    moved, pieces = refs[:n_moved], refs[n_moved:-4]
    total, count = acc.shape
    norm = jnp.zeros((count, 1), F32)
    start = 0
    for m in moved:
        for c in range(m.shape[1] // BLK):
            at = slice(start + c * BLK, start + (c + 1) * BLK)
            some = jnp.concatenate([p[:, at] for p in pieces], axis=0)
            part = lax.dot_general(
                m[:, c * BLK : (c + 1) * BLK], some, (((1,), (1,)), ((), ())), preferred_element_type=F32
            )
            acc[...] = acc[...] + part if at.start else part
            wide = some.astype(F32)
            norm += jnp.sum(wide * wide, axis=1, keepdims=True)
        start += m.shape[1]
    k = lax.broadcasted_iota(jnp.int32, (8, KPAD), 1)
    a, b = k // GRID - GRID // 2, k % GRID - GRID // 2
    cost = (a * a + b * b).astype(F32) * (0.5 / (OFFSET_SIGMA * OFFSET_SIGMA))
    pen = jnp.dot(
        jnp.where(k < OFFS, cost, 0.0).astype(BF16), one_hot(index_ref).astype(BF16), preferred_element_type=F32
    )
    rows = total // SHIFTS
    scores = acc[...].T - 0.5 * norm - pen[0:1, :]
    top = over_shifts(jnp.maximum, jnp.max(scores, axis=0, keepdims=True), rows)
    value = jnp.exp(scores - tile_shifts(top))
    raised[...] = value
    stats[0:1, :] = top
    stats[1:2, :] = over_shifts(jnp.add, jnp.sum(value, axis=0, keepdims=True), rows)


def score(pieces, moved, index_t):
    total = moved[0].shape[0]
    count = sum(p.shape[0] for p in pieces)
    return pl.pallas_call(
        functools.partial(score_kernel, len(moved)),
        in_specs=[VMEM] * (len(pieces) + len(moved) + 1),
        out_specs=[VMEM, VMEM],
        out_shape=[
            jax.ShapeDtypeStruct((count, total), F32),
            jax.ShapeDtypeStruct((2, total // SHIFTS), F32),
        ],
        scratch_shapes=[pltpu.VMEM((total, count), F32)],
        compiler_params=params(),
        cost_estimate=pl.CostEstimate(flops=2 * 10**9, bytes_accessed=12 << 20, transcendentals=1 << 17),
        name="score",
    )(*moved, *pieces, index_t)


def insert_kernel(scale, raised, s0, s1, s2, s3, hot, *rest):
    moved, (mine, other, evidence, weight) = rest[:-4], rest[-4:]
    tops = [s[0:1, :] for s in (s0, s1, s2, s3)]
    sums = [s[1:2, :] for s in (s0, s1, s2, s3)]
    top = functools.reduce(jnp.maximum, tops)
    total = functools.reduce(jnp.add, [b * jnp.exp(a - top) for a, b in zip(tops, sums)])
    evidence[...] = top + jnp.log(total)
    factor = jnp.exp(tops[0] - top) / total
    weight[...] = (raised[...] * tile_shifts(factor)).astype(BF16)
    blocked = [jnp.dot(hot[s], weight[...], preferred_element_type=F32).astype(BF16) for s in range(SEG)]
    parts = [m[:, s : s + BLK] for m in moved for s in range(0, m.shape[1], BLK)]
    acc = jnp.dot(
        jnp.concatenate(blocked, axis=1), jnp.concatenate(parts, axis=0), preferred_element_type=F32
    )
    mine[...] = acc[: VB // 2] * scale
    other[...] = (acc[VB // 2 :] * scale).astype(BF16)


def insert(raised, stats, hot, moved, scale):
    count, total = raised.shape
    rows = total // SHIFTS
    return pl.pallas_call(
        functools.partial(insert_kernel, scale),
        in_specs=[VMEM] * (2 + len(stats) + len(moved)),
        out_specs=[VMEM] * 3,
        out_shape=[
            jax.ShapeDtypeStruct((VB // 2, BLK), F32),
            jax.ShapeDtypeStruct((VB // 2, BLK), BF16),
            jax.ShapeDtypeStruct((1, rows), F32),
        ],
        scratch_shapes=[pltpu.VMEM((count, total), BF16)],
        compiler_params=params(),
        cost_estimate=pl.CostEstimate(flops=3 * 10**9, bytes_accessed=12 << 20, transcendentals=0),
        name="insert",
    )(raised, *stats, hot, *moved)


def gather(references, early, late):
    far = [lax.ppermute(references, "dom", receive_from(*d)) for d in FAR[1:]]
    far, early = lax.optimization_barrier((far, early()))
    own = jnp.concatenate([references, *far], axis=0)
    first = [lax.ppermute(own, "dom", receive_from(*d)) for d in NEAR[1:5]]
    up = first[2]
    second = [lax.ppermute(up, "dom", receive_from(*d)) for d in ((1, 0), (-1, 0), (0, 1))]
    return [own, *first, *second], (early, late())


def shards(images, shift_index, references, slot_blocks):
    rows = images.shape[0]
    scale = (rows * Z * Y * SEG / VB) ** (-0.5)
    index_t, table = shift_index.T, phase_parts()
    pieces, moved = gather(
        references,
        lambda: shift_images(images, index_t, table[:CUT], 0),
        lambda: shift_images(images, index_t, table[CUT:], CUT),
    )
    hot = place_slots(slot_blocks.T)
    raised, stats = score(pieces, moved, index_t)
    swap = [(0, 1), (1, 0)]
    everyone = [
        stats,
        lax.ppermute(stats, "core", swap),
        lax.ppermute(stats, "px", swap),
        lax.ppermute(stats, ("px", "core"), [(i, 3 - i) for i in range(4)]),
    ]
    mine, other, evidence = insert(raised, everyone, hot, moved, scale)
    paired = mine + lax.ppermute(other, "core", swap).astype(F32)
    sent = paired.astype(BF16).reshape(2 * Z * Y, VB // (4 * Z * Y), BLK)
    arrived = lax.all_to_all(sent, ("px", "dom"), 0, 0, tiled=True)
    return (jnp.sum(arrived.astype(F32), axis=0), evidence.reshape(rows))


def solution(mesh):
    split = Mesh(mesh.devices.reshape(2, 2, 2, Z * Y), ("half", "px", "core", "dom"))
    in_specs = (
        P(("half", "dom"), None),
        P(("half", "dom"), None),
        P(("half", "px", "core", "dom"), None),
        P(("half", "px", "core"), None),
    )
    out_specs = (P(("half", "px", "core", "dom"), None), P(("half", "dom")))
    return jax.shard_map(shards, mesh=split, in_specs=in_specs, out_specs=out_specs, check_vma=False)
```

```python
import functools
import math

import jax
import jax.numpy as jnp
import numpy as np
from jax import lax
from jax.experimental import pallas as pl
from jax.experimental.pallas import tpu as pltpu
from jax.sharding import Mesh
from jax.sharding import PartitionSpec as P

PIX = 64
SHIFTS = 9
GRID = 7
OFFS = GRID * GRID
KPAD = 112
CUT = 16
Z, Y = 8, 4
SEG = 8
BLK = 1024
VB = 256
OFFSET_SIGMA = 2.0
BF16 = jnp.bfloat16
F32 = jnp.float32


def dom_of(z, y):
    return (z % Z) * Y + y % Y


FAR = ((0, 0), (4, 0), (2, 2), (-2, 2))
NEAR = ((0, 0), (1, 0), (-1, 0), (0, 1), (0, -1), (1, 1), (-1, 1), (0, 2))


def receive_from(dz, dy):
    return [(dom_of(z + dz, y + dy), dom_of(z, y)) for z in range(Z) for y in range(Y)]


def phase_parts():
    offset = np.arange(OFFS)
    a, b = offset // GRID - GRID // 2, offset % GRID - GRID // 2
    f = np.arange(PIX) - PIX // 2
    turns = (f[:, None, None] * a[None, :, None] + f[None, None, :] * b[None, :, None]) % PIX
    angle = -2.0 * math.pi / PIX * turns
    cos, sin = np.cos(angle), np.sin(angle)
    table = np.concatenate([cos, cos, -sin, sin], axis=2).astype(np.float32)
    high = table.astype(BF16)
    low = (table - high.astype(np.float32)).astype(BF16)
    pad = np.zeros((PIX, KPAD - 2 * OFFS, 4 * PIX), BF16)
    return np.concatenate([high, low, pad], axis=1)


def one_hot(index_ref):
    rows = index_ref.shape[1]
    k = lax.broadcasted_iota(jnp.int32, (KPAD, rows), 0)
    offset = jnp.where(k < 2 * OFFS, k % OFFS, -1)
    return jnp.concatenate(
        [jnp.where(offset == index_ref[t : t + 1, :], 1.0, 0.0) for t in range(SHIFTS)], axis=1
    )


def shift_kernel(start, index_ref, image_ref, table_ref, out_ref, hot_ref):
    rows = image_ref.shape[0]
    hot_ref[...] = one_hot(index_ref).T.astype(BF16)
    for u in range(table_ref.shape[0]):
        phase = jnp.dot(hot_ref[...], table_ref[u], preferred_element_type=F32)
        cols = slice(u * 2 * PIX, (u + 1) * 2 * PIX)
        source = slice((start + u) * 2 * PIX, (start + u + 1) * 2 * PIX)
        x = image_ref[:, source].astype(F32)
        swapped = pltpu.roll(x, PIX, 1)
        for t in range(SHIFTS):
            part = phase[t * rows : (t + 1) * rows]
            out_ref[t * rows : (t + 1) * rows, cols] = (
                x * part[:, : 2 * PIX] + swapped * part[:, 2 * PIX :]
            ).astype(BF16)


VMEM = pl.BlockSpec(memory_space=pltpu.VMEM)


def params():
    return pltpu.CompilerParams(vmem_limit_bytes=24 << 20)


def shift_images(images, index_t, table, start):
    total = images.shape[0] * SHIFTS
    count = table.shape[0]
    return pl.pallas_call(
        functools.partial(shift_kernel, start),
        in_specs=[VMEM] * 3,
        out_specs=VMEM,
        out_shape=jax.ShapeDtypeStruct((total, count * 2 * PIX), BF16),
        scratch_shapes=[pltpu.VMEM((total, KPAD), BF16)],
        compiler_params=params(),
        cost_estimate=pl.CostEstimate(flops=count * 10**8, bytes_accessed=count << 18, transcendentals=0),
        name="shift",
    )(index_t, images, jnp.asarray(table))


def choose(g, values):
    out = jnp.zeros_like(g)
    for i, v in enumerate(values):
        if v:
            out = jnp.where(g == i, v, out)
    return out


def slots_kernel(slot_ref, hot_ref):
    count = slot_ref.shape[1]
    dom = lax.axis_index("dom")
    q = lax.broadcasted_iota(jnp.int32, (count, count), 1)
    piece, j = q // 16, (q // 4) % 4
    z = (dom // Y + choose(piece, [d for d, _ in NEAR]) + choose(j, [d for d, _ in FAR]) + Z) % Z
    y = (dom % Y + choose(piece, [d for _, d in NEAR]) + choose(j, [d for _, d in FAR]) + Y) % Y
    source = (z * Y + y) * 4 + q % 4
    order = jnp.where(lax.broadcasted_iota(jnp.int32, (count, count), 0) == source, 1.0, 0.0)
    slots = jnp.dot(
        slot_ref[...].astype(F32).astype(BF16), order.astype(BF16), preferred_element_type=F32
    ).astype(jnp.int32)
    core = lax.axis_index("core")
    m = lax.broadcasted_iota(jnp.int32, (VB, count), 0)
    half = m % (VB // 2)
    owner = jnp.where(m < VB // 2, core, 1 - core)
    block = (half // 2) % 2 * (VB // 2) + owner * (VB // 4) + half // 4 * 2 + half % 2
    for s in range(SEG):
        hot_ref[s] = jnp.where(block == slots[s : s + 1, :], 1.0, 0.0).astype(BF16)


def place_slots(slots_t):
    return pl.pallas_call(
        slots_kernel,
        in_specs=[VMEM],
        out_specs=VMEM,
        out_shape=jax.ShapeDtypeStruct((SEG, VB, slots_t.shape[1]), BF16),
        compiler_params=params(),
        cost_estimate=pl.CostEstimate(flops=10**8, bytes_accessed=4 << 20, transcendentals=0),
        name="slots",
    )(slots_t)


def tile_shifts(x):
    return jnp.concatenate([x] * SHIFTS, axis=1)


def over_shifts(op, x, rows):
    return functools.reduce(op, [x[:, t * rows : (t + 1) * rows] for t in range(SHIFTS)])


def score_kernel(n_moved, *refs):
    index_ref, raised, stats, acc = refs[-4:]
    moved, pieces = refs[:n_moved], refs[n_moved:-4]
    total, count = acc.shape
    norm = jnp.zeros((count, 1), F32)
    start = 0
    for m in moved:
        for c in range(m.shape[1] // BLK):
            at = slice(start + c * BLK, start + (c + 1) * BLK)
            some = jnp.concatenate([p[:, at] for p in pieces], axis=0)
            part = lax.dot_general(
                m[:, c * BLK : (c + 1) * BLK], some, (((1,), (1,)), ((), ())), preferred_element_type=F32
            )
            acc[...] = acc[...] + part if at.start else part
            wide = some.astype(F32)
            norm += jnp.sum(wide * wide, axis=1, keepdims=True)
        start += m.shape[1]
    k = lax.broadcasted_iota(jnp.int32, (8, KPAD), 1)
    a, b = k // GRID - GRID // 2, k % GRID - GRID // 2
    cost = (a * a + b * b).astype(F32) * (0.5 / (OFFSET_SIGMA * OFFSET_SIGMA))
    pen = jnp.dot(
        jnp.where(k < OFFS, cost, 0.0).astype(BF16), one_hot(index_ref).astype(BF16), preferred_element_type=F32
    )
    rows = total // SHIFTS
    scores = acc[...].T - 0.5 * norm - pen[0:1, :]
    top = over_shifts(jnp.maximum, jnp.max(scores, axis=0, keepdims=True), rows)
    value = jnp.exp(scores - tile_shifts(top))
    raised[...] = value
    stats[0:1, :] = top
    stats[1:2, :] = over_shifts(jnp.add, jnp.sum(value, axis=0, keepdims=True), rows)


def score(pieces, moved, index_t):
    total = moved[0].shape[0]
    count = sum(p.shape[0] for p in pieces)
    return pl.pallas_call(
        functools.partial(score_kernel, len(moved)),
        in_specs=[VMEM] * (len(pieces) + len(moved) + 1),
        out_specs=[VMEM, VMEM],
        out_shape=[
            jax.ShapeDtypeStruct((count, total), F32),
            jax.ShapeDtypeStruct((2, total // SHIFTS), F32),
        ],
        scratch_shapes=[pltpu.VMEM((total, count), F32)],
        compiler_params=params(),
        cost_estimate=pl.CostEstimate(flops=2 * 10**9, bytes_accessed=12 << 20, transcendentals=1 << 17),
        name="score",
    )(*moved, *pieces, index_t)


def insert_kernel(scale, raised, s0, s1, s2, s3, hot, *rest):
    moved, (mine, other, evidence, weight) = rest[:-4], rest[-4:]
    tops = [s[0:1, :] for s in (s0, s1, s2, s3)]
    sums = [s[1:2, :] for s in (s0, s1, s2, s3)]
    top = functools.reduce(jnp.maximum, tops)
    total = functools.reduce(jnp.add, [b * jnp.exp(a - top) for a, b in zip(tops, sums)])
    evidence[...] = top + jnp.log(total)
    factor = jnp.exp(tops[0] - top) / total
    weight[...] = (raised[...] * tile_shifts(factor)).astype(BF16)
    blocked = [jnp.dot(hot[s], weight[...], preferred_element_type=F32).astype(BF16) for s in range(SEG)]
    parts = [m[:, s : s + BLK] for m in moved for s in range(0, m.shape[1], BLK)]
    acc = jnp.dot(
        jnp.concatenate(blocked, axis=1), jnp.concatenate(parts, axis=0), preferred_element_type=F32
    )
    mine[...] = acc[: VB // 2] * scale
    other[...] = (acc[VB // 2 :] * scale).astype(BF16)


def insert(raised, stats, hot, moved, scale):
    count, total = raised.shape
    rows = total // SHIFTS
    return pl.pallas_call(
        functools.partial(insert_kernel, scale),
        in_specs=[VMEM] * (2 + len(stats) + len(moved)),
        out_specs=[VMEM] * 3,
        out_shape=[
            jax.ShapeDtypeStruct((VB // 2, BLK), F32),
            jax.ShapeDtypeStruct((VB // 2, BLK), BF16),
            jax.ShapeDtypeStruct((1, rows), F32),
        ],
        scratch_shapes=[pltpu.VMEM((count, total), BF16)],
        compiler_params=params(),
        cost_estimate=pl.CostEstimate(flops=3 * 10**9, bytes_accessed=12 << 20, transcendentals=0),
        name="insert",
    )(raised, *stats, hot, *moved)


def gather(references, early, late):
    far = [lax.ppermute(references, "dom", receive_from(*d)) for d in FAR[1:]]
    far, early = lax.optimization_barrier((far, early()))
    own = jnp.concatenate([references, *far], axis=0)
    first = [lax.ppermute(own, "dom", receive_from(*d)) for d in NEAR[1:5]]
    up = first[2]
    second = [lax.ppermute(up, "dom", receive_from(*d)) for d in ((1, 0), (-1, 0), (0, 1))]
    return [own, *first, *second], (early, late())


def shards(images, shift_index, references, slot_blocks):
    rows = images.shape[0]
    scale = (rows * Z * Y * SEG / VB) ** (-0.5)
    index_t, table = shift_index.T, phase_parts()
    pieces, moved = gather(
        references,
        lambda: shift_images(images, index_t, table[:CUT], 0),
        lambda: shift_images(images, index_t, table[CUT:], CUT),
    )
    hot = place_slots(slot_blocks.T)
    raised, stats = score(pieces, moved, index_t)
    swap = [(0, 1), (1, 0)]
    everyone = [
        stats,
        lax.ppermute(stats, ("px", "core"), [(i, 3 - i) for i in range(4)]),
        lax.ppermute(stats, "px", swap),
        lax.ppermute(stats, "core", swap),
    ]
    mine, other, evidence = insert(raised, everyone, hot, moved, scale)
    paired = mine + lax.ppermute(other, "core", swap).astype(F32)
    sent = paired.astype(BF16).reshape(2 * Z * Y, VB // (4 * Z * Y), BLK)
    arrived = lax.all_to_all(sent, ("dom", "px"), 0, 0, tiled=True)
    return (jnp.sum(arrived.astype(F32), axis=0), evidence.reshape(rows))


def solution(mesh):
    split = Mesh(mesh.devices.reshape(2, 2, 2, Z * Y), ("half", "px", "core", "dom"))
    in_specs = (
        P(("half", "dom"), None),
        P(("half", "dom"), None),
        P(("half", "px", "core", "dom"), None),
        P(("half", "px", "core"), None),
    )
    out_specs = (P(("half", "px", "core", "dom"), None), P(("half", "dom")))
    return jax.shard_map(shards, mesh=split, in_specs=in_specs, out_specs=out_specs, check_vma=False)
```

```python
import functools
import math

import jax
import jax.numpy as jnp
import numpy as np
from jax import lax
from jax.experimental import pallas as pl
from jax.experimental.pallas import tpu as pltpu
from jax.sharding import Mesh
from jax.sharding import PartitionSpec as P

PIX = 64
SHIFTS = 9
GRID = 7
OFFS = GRID * GRID
KPAD = 112
CUT = 16
Z, Y = 8, 4
SEG = 8
BLK = 1024
VB = 256
OFFSET_SIGMA = 2.0
BF16 = jnp.bfloat16
F32 = jnp.float32


def dom_of(z, y):
    return (z % Z) * Y + y % Y


FAR = ((0, 0), (4, 0), (2, 2), (-2, 2))
NEAR = ((0, 0), (1, 0), (-1, 0), (0, 1), (0, -1), (-2, 0), (-1, 1), (-1, -1))


def receive_from(dz, dy):
    return [(dom_of(z + dz, y + dy), dom_of(z, y)) for z in range(Z) for y in range(Y)]


def phase_parts():
    offset = np.arange(OFFS)
    a, b = offset // GRID - GRID // 2, offset % GRID - GRID // 2
    f = np.arange(PIX) - PIX // 2
    turns = (f[:, None, None] * a[None, :, None] + f[None, None, :] * b[None, :, None]) % PIX
    angle = -2.0 * math.pi / PIX * turns
    cos, sin = np.cos(angle), np.sin(angle)
    table = np.concatenate([cos, cos, -sin, sin], axis=2).astype(np.float32)
    high = table.astype(BF16)
    low = (table - high.astype(np.float32)).astype(BF16)
    pad = np.zeros((PIX, KPAD - 2 * OFFS, 4 * PIX), BF16)
    return np.concatenate([high, low, pad], axis=1)


def one_hot(index_ref):
    rows = index_ref.shape[1]
    k = lax.broadcasted_iota(jnp.int32, (KPAD, rows), 0)
    offset = jnp.where(k < 2 * OFFS, k % OFFS, -1)
    return jnp.concatenate(
        [jnp.where(offset == index_ref[t : t + 1, :], 1.0, 0.0) for t in range(SHIFTS)], axis=1
    )


def shift_kernel(start, index_ref, image_ref, table_ref, out_ref, hot_ref):
    rows = image_ref.shape[0]
    hot_ref[...] = one_hot(index_ref).T.astype(BF16)
    for u in range(table_ref.shape[0]):
        phase = jnp.dot(hot_ref[...], table_ref[u], preferred_element_type=F32)
        cols = slice(u * 2 * PIX, (u + 1) * 2 * PIX)
        source = slice((start + u) * 2 * PIX, (start + u + 1) * 2 * PIX)
        x = image_ref[:, source].astype(F32)
        swapped = pltpu.roll(x, PIX, 1)
        for t in range(SHIFTS):
            part = phase[t * rows : (t + 1) * rows]
            out_ref[t * rows : (t + 1) * rows, cols] = (
                x * part[:, : 2 * PIX] + swapped * part[:, 2 * PIX :]
            ).astype(BF16)


VMEM = pl.BlockSpec(memory_space=pltpu.VMEM)


def params():
    return pltpu.CompilerParams(vmem_limit_bytes=24 << 20)


def shift_images(images, index_t, table, start):
    total = images.shape[0] * SHIFTS
    count = table.shape[0]
    return pl.pallas_call(
        functools.partial(shift_kernel, start),
        in_specs=[VMEM] * 3,
        out_specs=VMEM,
        out_shape=jax.ShapeDtypeStruct((total, count * 2 * PIX), BF16),
        scratch_shapes=[pltpu.VMEM((total, KPAD), BF16)],
        compiler_params=params(),
        cost_estimate=pl.CostEstimate(flops=count * 10**8, bytes_accessed=count << 18, transcendentals=0),
        name="shift",
    )(index_t, images, jnp.asarray(table))


def choose(g, values):
    out = jnp.zeros_like(g)
    for i, v in enumerate(values):
        if v:
            out = jnp.where(g == i, v, out)
    return out


def slots_kernel(slot_ref, hot_ref):
    count = slot_ref.shape[1]
    dom = lax.axis_index("dom")
    q = lax.broadcasted_iota(jnp.int32, (count, count), 1)
    piece, j = q // 16, (q // 4) % 4
    z = (dom // Y + choose(piece, [d for d, _ in NEAR]) + choose(j, [d for d, _ in FAR]) + Z) % Z
    y = (dom % Y + choose(piece, [d for _, d in NEAR]) + choose(j, [d for _, d in FAR]) + Y) % Y
    source = (z * Y + y) * 4 + q % 4
    order = jnp.where(lax.broadcasted_iota(jnp.int32, (count, count), 0) == source, 1.0, 0.0)
    slots = jnp.dot(
        slot_ref[...].astype(F32).astype(BF16), order.astype(BF16), preferred_element_type=F32
    ).astype(jnp.int32)
    core = lax.axis_index("core")
    m = lax.broadcasted_iota(jnp.int32, (VB, count), 0)
    half = m % (VB // 2)
    owner = jnp.where(m < VB // 2, core, 1 - core)
    block = (half // 2) % 2 * (VB // 2) + owner * (VB // 4) + half // 4 * 2 + half % 2
    for s in range(SEG):
        hot_ref[s] = jnp.where(block == slots[s : s + 1, :], 1.0, 0.0).astype(BF16)


def place_slots(slots_t):
    return pl.pallas_call(
        slots_kernel,
        in_specs=[VMEM],
        out_specs=VMEM,
        out_shape=jax.ShapeDtypeStruct((SEG, VB, slots_t.shape[1]), BF16),
        compiler_params=params(),
        cost_estimate=pl.CostEstimate(flops=10**8, bytes_accessed=4 << 20, transcendentals=0),
        name="slots",
    )(slots_t)


def tile_shifts(x):
    return jnp.concatenate([x] * SHIFTS, axis=1)


def over_shifts(op, x, rows):
    return functools.reduce(op, [x[:, t * rows : (t + 1) * rows] for t in range(SHIFTS)])


def score_kernel(n_moved, *refs):
    index_ref, raised, stats, acc = refs[-4:]
    moved, pieces = refs[:n_moved], refs[n_moved:-4]
    total, count = acc.shape
    norm = jnp.zeros((count, 1), F32)
    start = 0
    for m in moved:
        for c in range(m.shape[1] // BLK):
            at = slice(start + c * BLK, start + (c + 1) * BLK)
            some = jnp.concatenate([p[:, at] for p in pieces], axis=0)
            part = lax.dot_general(
                m[:, c * BLK : (c + 1) * BLK], some, (((1,), (1,)), ((), ())), preferred_element_type=F32
            )
            acc[...] = acc[...] + part if at.start else part
            wide = some.astype(F32)
            norm += jnp.sum(wide * wide, axis=1, keepdims=True)
        start += m.shape[1]
    k = lax.broadcasted_iota(jnp.int32, (8, KPAD), 1)
    a, b = k // GRID - GRID // 2, k % GRID - GRID // 2
    cost = (a * a + b * b).astype(F32) * (0.5 / (OFFSET_SIGMA * OFFSET_SIGMA))
    pen = jnp.dot(
        jnp.where(k < OFFS, cost, 0.0).astype(BF16), one_hot(index_ref).astype(BF16), preferred_element_type=F32
    )
    rows = total // SHIFTS
    scores = acc[...].T - 0.5 * norm - pen[0:1, :]
    top = over_shifts(jnp.maximum, jnp.max(scores, axis=0, keepdims=True), rows)
    value = jnp.exp(scores - tile_shifts(top))
    raised[...] = value
    stats[0:1, :] = top
    stats[1:2, :] = over_shifts(jnp.add, jnp.sum(value, axis=0, keepdims=True), rows)


def score(pieces, moved, index_t):
    total = moved[0].shape[0]
    count = sum(p.shape[0] for p in pieces)
    return pl.pallas_call(
        functools.partial(score_kernel, len(moved)),
        in_specs=[VMEM] * (len(pieces) + len(moved) + 1),
        out_specs=[VMEM, VMEM],
        out_shape=[
            jax.ShapeDtypeStruct((count, total), F32),
            jax.ShapeDtypeStruct((2, total // SHIFTS), F32),
        ],
        scratch_shapes=[pltpu.VMEM((total, count), F32)],
        compiler_params=params(),
        cost_estimate=pl.CostEstimate(flops=2 * 10**9, bytes_accessed=12 << 20, transcendentals=1 << 17),
        name="score",
    )(*moved, *pieces, index_t)


def insert_kernel(scale, raised, s0, s1, s2, s3, hot, *rest):
    moved, (mine, other, evidence, weight) = rest[:-4], rest[-4:]
    tops = [s[0:1, :] for s in (s0, s1, s2, s3)]
    sums = [s[1:2, :] for s in (s0, s1, s2, s3)]
    top = functools.reduce(jnp.maximum, tops)
    total = functools.reduce(jnp.add, [b * jnp.exp(a - top) for a, b in zip(tops, sums)])
    evidence[...] = top + jnp.log(total)
    factor = jnp.exp(tops[0] - top) / total
    weight[...] = (raised[...] * tile_shifts(factor)).astype(BF16)
    blocked = [jnp.dot(hot[s], weight[...], preferred_element_type=F32).astype(BF16) for s in range(SEG)]
    parts = [m[:, s : s + BLK] for m in moved for s in range(0, m.shape[1], BLK)]
    acc = jnp.dot(
        jnp.concatenate(blocked, axis=1), jnp.concatenate(parts, axis=0), preferred_element_type=F32
    )
    mine[...] = acc[: VB // 2] * scale
    other[...] = (acc[VB // 2 :] * scale).astype(BF16)


def insert(raised, stats, hot, moved, scale):
    count, total = raised.shape
    rows = total // SHIFTS
    return pl.pallas_call(
        functools.partial(insert_kernel, scale),
        in_specs=[VMEM] * (2 + len(stats) + len(moved)),
        out_specs=[VMEM] * 3,
        out_shape=[
            jax.ShapeDtypeStruct((VB // 2, BLK), F32),
            jax.ShapeDtypeStruct((VB // 2, BLK), BF16),
            jax.ShapeDtypeStruct((1, rows), F32),
        ],
        scratch_shapes=[pltpu.VMEM((count, total), BF16)],
        compiler_params=params(),
        cost_estimate=pl.CostEstimate(flops=3 * 10**9, bytes_accessed=12 << 20, transcendentals=0),
        name="insert",
    )(raised, *stats, hot, *moved)


def gather(references, early, late):
    far = [lax.ppermute(references, "dom", receive_from(*d)) for d in FAR[1:]]
    far, early = lax.optimization_barrier((far, early()))
    own = jnp.concatenate([references, *far], axis=0)
    first = [lax.ppermute(own, "dom", receive_from(*d)) for d in NEAR[1:5]]
    up = first[1]
    second = [lax.ppermute(up, "dom", receive_from(*d)) for d in ((-1, 0), (0, 1), (0, -1))]
    return [own, *first, *second], (early, late())


def shards(images, shift_index, references, slot_blocks):
    rows = images.shape[0]
    scale = (rows * Z * Y * SEG / VB) ** (-0.5)
    index_t, table = shift_index.T, phase_parts()
    pieces, moved = gather(
        references,
        lambda: shift_images(images, index_t, table[:CUT], 0),
        lambda: shift_images(images, index_t, table[CUT:], CUT),
    )
    hot = place_slots(slot_blocks.T)
    raised, stats = score(pieces, moved, index_t)
    swap = [(0, 1), (1, 0)]
    everyone = [
        stats,
        lax.ppermute(stats, ("px", "core"), [(i, 3 - i) for i in range(4)]),
        lax.ppermute(stats, "px", swap),
        lax.ppermute(stats, "core", swap),
    ]
    mine, other, evidence = insert(raised, everyone, hot, moved, scale)
    paired = mine + lax.ppermute(other, "core", swap).astype(F32)
    sent = paired.astype(BF16).reshape(2 * Z * Y, VB // (4 * Z * Y), BLK)
    arrived = lax.all_to_all(sent, ("dom", "px"), 0, 0, tiled=True)
    return (jnp.sum(arrived.astype(F32), axis=0), evidence.reshape(rows))


def solution(mesh):
    split = Mesh(mesh.devices.reshape(2, 2, 2, Z * Y), ("half", "px", "core", "dom"))
    in_specs = (
        P(("half", "dom"), None),
        P(("half", "dom"), None),
        P(("half", "px", "core", "dom"), None),
        P(("half", "px", "core"), None),
    )
    out_specs = (P(("half", "px", "core", "dom"), None), P(("half", "dom")))
    return jax.shard_map(shards, mesh=split, in_specs=in_specs, out_specs=out_specs, check_vma=False)
```

```python
import functools
import math

import jax
import jax.numpy as jnp
import numpy as np
from jax import lax
from jax.experimental import pallas as pl
from jax.experimental.pallas import tpu as pltpu
from jax.sharding import Mesh
from jax.sharding import PartitionSpec as P

PIX = 64
SHIFTS = 9
GRID = 7
OFFS = GRID * GRID
KPAD = 112
CUT = 16
Z, Y = 8, 4
SEG = 8
BLK = 1024
VB = 256
OFFSET_SIGMA = 2.0
BF16 = jnp.bfloat16
F32 = jnp.float32


def dom_of(z, y):
    return (z % Z) * Y + y % Y


FAR = ((0, 0), (4, 0), (2, 2), (-2, 2))
NEAR = ((0, 0), (-1, 0), (0, 1), (0, -1), (1, 0), (-2, 0), (-1, 1), (-1, -1))


def receive_from(dz, dy):
    return [(dom_of(z + dz, y + dy), dom_of(z, y)) for z in range(Z) for y in range(Y)]


def phase_parts():
    offset = np.arange(OFFS)
    a, b = offset // GRID - GRID // 2, offset % GRID - GRID // 2
    f = np.arange(PIX) - PIX // 2
    turns = (f[:, None, None] * a[None, :, None] + f[None, None, :] * b[None, :, None]) % PIX
    angle = -2.0 * math.pi / PIX * turns
    cos, sin = np.cos(angle), np.sin(angle)
    table = np.concatenate([cos, cos, -sin, sin], axis=2).astype(np.float32)
    high = table.astype(BF16)
    low = (table - high.astype(np.float32)).astype(BF16)
    pad = np.zeros((PIX, KPAD - 2 * OFFS, 4 * PIX), BF16)
    return np.concatenate([high, low, pad], axis=1)


def one_hot(index_ref):
    rows = index_ref.shape[1]
    k = lax.broadcasted_iota(jnp.int32, (KPAD, rows), 0)
    offset = jnp.where(k < 2 * OFFS, k % OFFS, -1)
    return jnp.concatenate(
        [jnp.where(offset == index_ref[t : t + 1, :], 1.0, 0.0) for t in range(SHIFTS)], axis=1
    )


def shift_kernel(start, index_ref, image_ref, table_ref, out_ref, hot_ref):
    rows = image_ref.shape[0]
    hot_ref[...] = one_hot(index_ref).T.astype(BF16)
    for u in range(table_ref.shape[0]):
        phase = jnp.dot(hot_ref[...], table_ref[u], preferred_element_type=F32)
        cols = slice(u * 2 * PIX, (u + 1) * 2 * PIX)
        source = slice((start + u) * 2 * PIX, (start + u + 1) * 2 * PIX)
        x = image_ref[:, source].astype(F32)
        swapped = pltpu.roll(x, PIX, 1)
        for t in range(SHIFTS):
            part = phase[t * rows : (t + 1) * rows]
            out_ref[t * rows : (t + 1) * rows, cols] = (
                x * part[:, : 2 * PIX] + swapped * part[:, 2 * PIX :]
            ).astype(BF16)


VMEM = pl.BlockSpec(memory_space=pltpu.VMEM)


def params():
    return pltpu.CompilerParams(vmem_limit_bytes=24 << 20)


def shift_images(images, index_t, table, start):
    total = images.shape[0] * SHIFTS
    count = table.shape[0]
    return pl.pallas_call(
        functools.partial(shift_kernel, start),
        in_specs=[VMEM] * 3,
        out_specs=VMEM,
        out_shape=jax.ShapeDtypeStruct((total, count * 2 * PIX), BF16),
        scratch_shapes=[pltpu.VMEM((total, KPAD), BF16)],
        compiler_params=params(),
        cost_estimate=pl.CostEstimate(flops=count * 10**8, bytes_accessed=count << 18, transcendentals=0),
        name="shift",
    )(index_t, images, jnp.asarray(table))


def choose(g, values):
    out = jnp.zeros_like(g)
    for i, v in enumerate(values):
        if v:
            out = jnp.where(g == i, v, out)
    return out


def slots_kernel(slot_ref, hot_ref):
    count = slot_ref.shape[1]
    dom = lax.axis_index("dom")
    q = lax.broadcasted_iota(jnp.int32, (count, count), 1)
    piece, j = q // 16, (q // 4) % 4
    z = (dom // Y + choose(piece, [d for d, _ in NEAR]) + choose(j, [d for d, _ in FAR]) + Z) % Z
    y = (dom % Y + choose(piece, [d for _, d in NEAR]) + choose(j, [d for _, d in FAR]) + Y) % Y
    source = (z * Y + y) * 4 + q % 4
    order = jnp.where(lax.broadcasted_iota(jnp.int32, (count, count), 0) == source, 1.0, 0.0)
    slots = jnp.dot(
        slot_ref[...].astype(F32).astype(BF16), order.astype(BF16), preferred_element_type=F32
    ).astype(jnp.int32)
    core = lax.axis_index("core")
    m = lax.broadcasted_iota(jnp.int32, (VB, count), 0)
    half = m % (VB // 2)
    owner = jnp.where(m < VB // 2, core, 1 - core)
    block = (half // 2) % 2 * (VB // 2) + owner * (VB // 4) + half // 4 * 2 + half % 2
    for s in range(SEG):
        hot_ref[s] = jnp.where(block == slots[s : s + 1, :], 1.0, 0.0).astype(BF16)


def place_slots(slots_t):
    return pl.pallas_call(
        slots_kernel,
        in_specs=[VMEM],
        out_specs=VMEM,
        out_shape=jax.ShapeDtypeStruct((SEG, VB, slots_t.shape[1]), BF16),
        compiler_params=params(),
        cost_estimate=pl.CostEstimate(flops=10**8, bytes_accessed=4 << 20, transcendentals=0),
        name="slots",
    )(slots_t)


def tile_shifts(x):
    return jnp.concatenate([x] * SHIFTS, axis=1)


def over_shifts(op, x, rows):
    return functools.reduce(op, [x[:, t * rows : (t + 1) * rows] for t in range(SHIFTS)])


def score_kernel(n_moved, *refs):
    index_ref, raised, stats, acc = refs[-4:]
    moved, pieces = refs[:n_moved], refs[n_moved:-4]
    total, count = acc.shape
    norm = jnp.zeros((count, 1), F32)
    start = 0
    for m in moved:
        for c in range(m.shape[1] // BLK):
            at = slice(start + c * BLK, start + (c + 1) * BLK)
            some = jnp.concatenate([p[:, at] for p in pieces], axis=0)
            part = lax.dot_general(
                m[:, c * BLK : (c + 1) * BLK], some, (((1,), (1,)), ((), ())), preferred_element_type=F32
            )
            acc[...] = acc[...] + part if at.start else part
            wide = some.astype(F32)
            norm += jnp.sum(wide * wide, axis=1, keepdims=True)
        start += m.shape[1]
    k = lax.broadcasted_iota(jnp.int32, (8, KPAD), 1)
    a, b = k // GRID - GRID // 2, k % GRID - GRID // 2
    cost = (a * a + b * b).astype(F32) * (0.5 / (OFFSET_SIGMA * OFFSET_SIGMA))
    pen = jnp.dot(
        jnp.where(k < OFFS, cost, 0.0).astype(BF16), one_hot(index_ref).astype(BF16), preferred_element_type=F32
    )
    rows = total // SHIFTS
    scores = acc[...].T - 0.5 * norm - pen[0:1, :]
    top = over_shifts(jnp.maximum, jnp.max(scores, axis=0, keepdims=True), rows)
    value = jnp.exp(scores - tile_shifts(top))
    raised[...] = value
    stats[0:1, :] = top
    stats[1:2, :] = over_shifts(jnp.add, jnp.sum(value, axis=0, keepdims=True), rows)


def score(pieces, moved, index_t):
    total = moved[0].shape[0]
    count = sum(p.shape[0] for p in pieces)
    return pl.pallas_call(
        functools.partial(score_kernel, len(moved)),
        in_specs=[VMEM] * (len(pieces) + len(moved) + 1),
        out_specs=[VMEM, VMEM],
        out_shape=[
            jax.ShapeDtypeStruct((count, total), F32),
            jax.ShapeDtypeStruct((2, total // SHIFTS), F32),
        ],
        scratch_shapes=[pltpu.VMEM((total, count), F32)],
        compiler_params=params(),
        cost_estimate=pl.CostEstimate(flops=2 * 10**9, bytes_accessed=12 << 20, transcendentals=1 << 17),
        name="score",
    )(*moved, *pieces, index_t)


def insert_kernel(scale, raised, s0, s1, s2, s3, hot, *rest):
    moved, (mine, other, evidence, weight) = rest[:-4], rest[-4:]
    tops = [s[0:1, :] for s in (s0, s1, s2, s3)]
    sums = [s[1:2, :] for s in (s0, s1, s2, s3)]
    top = functools.reduce(jnp.maximum, tops)
    total = functools.reduce(jnp.add, [b * jnp.exp(a - top) for a, b in zip(tops, sums)])
    evidence[...] = top + jnp.log(total)
    factor = jnp.exp(tops[0] - top) / total
    weight[...] = (raised[...] * tile_shifts(factor)).astype(BF16)
    blocked = [jnp.dot(hot[s], weight[...], preferred_element_type=F32).astype(BF16) for s in range(SEG)]
    parts = [m[:, s : s + BLK] for m in moved for s in range(0, m.shape[1], BLK)]
    acc = jnp.dot(
        jnp.concatenate(blocked, axis=1), jnp.concatenate(parts, axis=0), preferred_element_type=F32
    )
    mine[...] = acc[: VB // 2] * scale
    other[...] = (acc[VB // 2 :] * scale).astype(BF16)


def insert(raised, stats, hot, moved, scale):
    count, total = raised.shape
    rows = total // SHIFTS
    return pl.pallas_call(
        functools.partial(insert_kernel, scale),
        in_specs=[VMEM] * (2 + len(stats) + len(moved)),
        out_specs=[VMEM] * 3,
        out_shape=[
            jax.ShapeDtypeStruct((VB // 2, BLK), F32),
            jax.ShapeDtypeStruct((VB // 2, BLK), BF16),
            jax.ShapeDtypeStruct((1, rows), F32),
        ],
        scratch_shapes=[pltpu.VMEM((count, total), BF16)],
        compiler_params=params(),
        cost_estimate=pl.CostEstimate(flops=3 * 10**9, bytes_accessed=12 << 20, transcendentals=0),
        name="insert",
    )(raised, *stats, hot, *moved)


def gather(references, early, late):
    far = [lax.ppermute(references, "dom", receive_from(*d)) for d in FAR[1:]]
    far, early = lax.optimization_barrier((far, early()))
    own = jnp.concatenate([references, *far], axis=0)
    first = [lax.ppermute(own, "dom", receive_from(*d)) for d in NEAR[1:5]]
    up = first[0]
    second = [lax.ppermute(up, "dom", receive_from(*d)) for d in ((-1, 0), (0, 1), (0, -1))]
    return [own, *first, *second], (early, late())


def shards(images, shift_index, references, slot_blocks):
    rows = images.shape[0]
    scale = (rows * Z * Y * SEG / VB) ** (-0.5)
    index_t, table = shift_index.T, phase_parts()
    pieces, moved = gather(
        references,
        lambda: shift_images(images, index_t, table[:CUT], 0),
        lambda: shift_images(images, index_t, table[CUT:], CUT),
    )
    hot = place_slots(slot_blocks.T)
    raised, stats = score(pieces, moved, index_t)
    swap = [(0, 1), (1, 0)]
    everyone = [
        stats,
        lax.ppermute(stats, ("px", "core"), [(i, 3 - i) for i in range(4)]),
        lax.ppermute(stats, "px", swap),
        lax.ppermute(stats, "core", swap),
    ]
    mine, other, evidence = insert(raised, everyone, hot, moved, scale)
    paired = mine + lax.ppermute(other, "core", swap).astype(F32)
    sent = paired.astype(BF16).reshape(2 * Z * Y, VB // (4 * Z * Y), BLK)
    arrived = lax.all_to_all(sent, ("dom", "px"), 0, 0, tiled=True)
    return (jnp.sum(arrived.astype(F32), axis=0), evidence.reshape(rows))


def solution(mesh):
    split = Mesh(mesh.devices.reshape(2, 2, 2, Z * Y), ("half", "px", "core", "dom"))
    in_specs = (
        P(("half", "dom"), None),
        P(("half", "dom"), None),
        P(("half", "px", "core", "dom"), None),
        P(("half", "px", "core"), None),
    )
    out_specs = (P(("half", "px", "core", "dom"), None), P(("half", "dom")))
    return jax.shard_map(shards, mesh=split, in_specs=in_specs, out_specs=out_specs, check_vma=False)
```

```python
import functools
import math

import jax
import jax.numpy as jnp
import numpy as np
from jax import lax
from jax.experimental import pallas as pl
from jax.experimental.pallas import tpu as pltpu
from jax.sharding import Mesh
from jax.sharding import PartitionSpec as P

PIX = 64
SHIFTS = 9
GRID = 7
OFFS = GRID * GRID
KPAD = 112
CUT = 16
Z, Y = 8, 4
SEG = 8
BLK = 1024
VB = 256
OFFSET_SIGMA = 2.0
BF16 = jnp.bfloat16
F32 = jnp.float32


def dom_of(z, y):
    return (z % Z) * Y + y % Y


FAR = ((0, 0), (2, 2), (-2, 2), (4, 0))
NEAR = ((0, 0), (-1, 0), (0, 1), (0, -1), (1, 0), (-2, 0), (-1, 1), (-1, -1))


def receive_from(dz, dy):
    return [(dom_of(z + dz, y + dy), dom_of(z, y)) for z in range(Z) for y in range(Y)]


def phase_parts():
    offset = np.arange(OFFS)
    a, b = offset // GRID - GRID // 2, offset % GRID - GRID // 2
    f = np.arange(PIX) - PIX // 2
    turns = (f[:, None, None] * a[None, :, None] + f[None, None, :] * b[None, :, None]) % PIX
    angle = -2.0 * math.pi / PIX * turns
    cos, sin = np.cos(angle), np.sin(angle)
    table = np.concatenate([cos, cos, -sin, sin], axis=2).astype(np.float32)
    high = table.astype(BF16)
    low = (table - high.astype(np.float32)).astype(BF16)
    pad = np.zeros((PIX, KPAD - 2 * OFFS, 4 * PIX), BF16)
    return np.concatenate([high, low, pad], axis=1)


def one_hot(index_ref):
    rows = index_ref.shape[1]
    k = lax.broadcasted_iota(jnp.int32, (KPAD, rows), 0)
    offset = jnp.where(k < 2 * OFFS, k % OFFS, -1)
    return jnp.concatenate(
        [jnp.where(offset == index_ref[t : t + 1, :], 1.0, 0.0) for t in range(SHIFTS)], axis=1
    )


def shift_kernel(start, index_ref, image_ref, table_ref, out_ref, hot_ref):
    rows = image_ref.shape[0]
    hot_ref[...] = one_hot(index_ref).T.astype(BF16)
    for u in range(table_ref.shape[0]):
        phase = jnp.dot(hot_ref[...], table_ref[u], preferred_element_type=F32)
        cols = slice(u * 2 * PIX, (u + 1) * 2 * PIX)
        source = slice((start + u) * 2 * PIX, (start + u + 1) * 2 * PIX)
        x = image_ref[:, source].astype(F32)
        swapped = pltpu.roll(x, PIX, 1)
        for t in range(SHIFTS):
            part = phase[t * rows : (t + 1) * rows]
            out_ref[t * rows : (t + 1) * rows, cols] = (
                x * part[:, : 2 * PIX] + swapped * part[:, 2 * PIX :]
            ).astype(BF16)


VMEM = pl.BlockSpec(memory_space=pltpu.VMEM)


def params():
    return pltpu.CompilerParams(vmem_limit_bytes=24 << 20)


def shift_images(images, index_t, table, start):
    total = images.shape[0] * SHIFTS
    count = table.shape[0]
    return pl.pallas_call(
        functools.partial(shift_kernel, start),
        in_specs=[VMEM] * 3,
        out_specs=VMEM,
        out_shape=jax.ShapeDtypeStruct((total, count * 2 * PIX), BF16),
        scratch_shapes=[pltpu.VMEM((total, KPAD), BF16)],
        compiler_params=params(),
        cost_estimate=pl.CostEstimate(flops=count * 10**8, bytes_accessed=count << 18, transcendentals=0),
        name="shift",
    )(index_t, images, jnp.asarray(table))


def choose(g, values):
    out = jnp.zeros_like(g)
    for i, v in enumerate(values):
        if v:
            out = jnp.where(g == i, v, out)
    return out


def slots_kernel(slot_ref, hot_ref):
    count = slot_ref.shape[1]
    dom = lax.axis_index("dom")
    q = lax.broadcasted_iota(jnp.int32, (count, count), 1)
    piece, j = q // 16, (q // 4) % 4
    z = (dom // Y + choose(piece, [d for d, _ in NEAR]) + choose(j, [d for d, _ in FAR]) + Z) % Z
    y = (dom % Y + choose(piece, [d for _, d in NEAR]) + choose(j, [d for _, d in FAR]) + Y) % Y
    source = (z * Y + y) * 4 + q % 4
    order = jnp.where(lax.broadcasted_iota(jnp.int32, (count, count), 0) == source, 1.0, 0.0)
    slots = jnp.dot(
        slot_ref[...].astype(F32).astype(BF16), order.astype(BF16), preferred_element_type=F32
    ).astype(jnp.int32)
    core = lax.axis_index("core")
    m = lax.broadcasted_iota(jnp.int32, (VB, count), 0)
    half = m % (VB // 2)
    owner = jnp.where(m < VB // 2, core, 1 - core)
    block = (half // 2) % 2 * (VB // 2) + owner * (VB // 4) + half // 4 * 2 + half % 2
    for s in range(SEG):
        hot_ref[s] = jnp.where(block == slots[s : s + 1, :], 1.0, 0.0).astype(BF16)


def place_slots(slots_t):
    return pl.pallas_call(
        slots_kernel,
        in_specs=[VMEM],
        out_specs=VMEM,
        out_shape=jax.ShapeDtypeStruct((SEG, VB, slots_t.shape[1]), BF16),
        compiler_params=params(),
        cost_estimate=pl.CostEstimate(flops=10**8, bytes_accessed=4 << 20, transcendentals=0),
        name="slots",
    )(slots_t)


def tile_shifts(x):
    return jnp.concatenate([x] * SHIFTS, axis=1)


def over_shifts(op, x, rows):
    return functools.reduce(op, [x[:, t * rows : (t + 1) * rows] for t in range(SHIFTS)])


def score_kernel(n_moved, *refs):
    index_ref, raised, stats, acc = refs[-4:]
    moved, pieces = refs[:n_moved], refs[n_moved:-4]
    total, count = acc.shape
    norm = jnp.zeros((count, 1), F32)
    start = 0
    for m in moved:
        for c in range(m.shape[1] // BLK):
            at = slice(start + c * BLK, start + (c + 1) * BLK)
            some = jnp.concatenate([p[:, at] for p in pieces], axis=0)
            part = lax.dot_general(
                m[:, c * BLK : (c + 1) * BLK], some, (((1,), (1,)), ((), ())), preferred_element_type=F32
            )
            acc[...] = acc[...] + part if at.start else part
            wide = some.astype(F32)
            norm += jnp.sum(wide * wide, axis=1, keepdims=True)
        start += m.shape[1]
    k = lax.broadcasted_iota(jnp.int32, (8, KPAD), 1)
    a, b = k // GRID - GRID // 2, k % GRID - GRID // 2
    cost = (a * a + b * b).astype(F32) * (0.5 / (OFFSET_SIGMA * OFFSET_SIGMA))
    pen = jnp.dot(
        jnp.where(k < OFFS, cost, 0.0).astype(BF16), one_hot(index_ref).astype(BF16), preferred_element_type=F32
    )
    rows = total // SHIFTS
    scores = acc[...].T - 0.5 * norm - pen[0:1, :]
    top = over_shifts(jnp.maximum, jnp.max(scores, axis=0, keepdims=True), rows)
    value = jnp.exp(scores - tile_shifts(top))
    raised[...] = value
    stats[0:1, :] = top
    stats[1:2, :] = over_shifts(jnp.add, jnp.sum(value, axis=0, keepdims=True), rows)


def score(pieces, moved, index_t):
    total = moved[0].shape[0]
    count = sum(p.shape[0] for p in pieces)
    return pl.pallas_call(
        functools.partial(score_kernel, len(moved)),
        in_specs=[VMEM] * (len(pieces) + len(moved) + 1),
        out_specs=[VMEM, VMEM],
        out_shape=[
            jax.ShapeDtypeStruct((count, total), F32),
            jax.ShapeDtypeStruct((2, total // SHIFTS), F32),
        ],
        scratch_shapes=[pltpu.VMEM((total, count), F32)],
        compiler_params=params(),
        cost_estimate=pl.CostEstimate(flops=2 * 10**9, bytes_accessed=12 << 20, transcendentals=1 << 17),
        name="score",
    )(*moved, *pieces, index_t)


def insert_kernel(scale, raised, s0, s1, s2, s3, hot, *rest):
    moved, (mine, other, evidence, weight) = rest[:-4], rest[-4:]
    tops = [s[0:1, :] for s in (s0, s1, s2, s3)]
    sums = [s[1:2, :] for s in (s0, s1, s2, s3)]
    top = functools.reduce(jnp.maximum, tops)
    total = functools.reduce(jnp.add, [b * jnp.exp(a - top) for a, b in zip(tops, sums)])
    evidence[...] = top + jnp.log(total)
    factor = jnp.exp(tops[0] - top) / total
    weight[...] = (raised[...] * tile_shifts(factor)).astype(BF16)
    blocked = [jnp.dot(hot[s], weight[...], preferred_element_type=F32).astype(BF16) for s in range(SEG)]
    parts = [m[:, s : s + BLK] for m in moved for s in range(0, m.shape[1], BLK)]
    acc = jnp.dot(
        jnp.concatenate(blocked, axis=1), jnp.concatenate(parts, axis=0), preferred_element_type=F32
    )
    mine[...] = acc[: VB // 2] * scale
    other[...] = (acc[VB // 2 :] * scale).astype(BF16)


def insert(raised, stats, hot, moved, scale):
    count, total = raised.shape
    rows = total // SHIFTS
    return pl.pallas_call(
        functools.partial(insert_kernel, scale),
        in_specs=[VMEM] * (2 + len(stats) + len(moved)),
        out_specs=[VMEM] * 3,
        out_shape=[
            jax.ShapeDtypeStruct((VB // 2, BLK), F32),
            jax.ShapeDtypeStruct((VB // 2, BLK), BF16),
            jax.ShapeDtypeStruct((1, rows), F32),
        ],
        scratch_shapes=[pltpu.VMEM((count, total), BF16)],
        compiler_params=params(),
        cost_estimate=pl.CostEstimate(flops=3 * 10**9, bytes_accessed=12 << 20, transcendentals=0),
        name="insert",
    )(raised, *stats, hot, *moved)


def gather(references, early, late):
    far = [lax.ppermute(references, "dom", receive_from(*d)) for d in FAR[1:]]
    far, early = lax.optimization_barrier((far, early()))
    own = jnp.concatenate([references, *far], axis=0)
    first = [lax.ppermute(own, "dom", receive_from(*d)) for d in NEAR[1:5]]
    up = first[0]
    second = [lax.ppermute(up, "dom", receive_from(*d)) for d in ((-1, 0), (0, 1), (0, -1))]
    return [own, *first, *second], (early, late())


def shards(images, shift_index, references, slot_blocks):
    rows = images.shape[0]
    scale = (rows * Z * Y * SEG / VB) ** (-0.5)
    index_t, table = shift_index.T, phase_parts()
    pieces, moved = gather(
        references,
        lambda: shift_images(images, index_t, table[:CUT], 0),
        lambda: shift_images(images, index_t, table[CUT:], CUT),
    )
    hot = place_slots(slot_blocks.T)
    raised, stats = score(pieces, moved, index_t)
    swap = [(0, 1), (1, 0)]
    everyone = [
        stats,
        lax.ppermute(stats, ("px", "core"), [(i, 3 - i) for i in range(4)]),
        lax.ppermute(stats, "px", swap),
        lax.ppermute(stats, "core", swap),
    ]
    mine, other, evidence = insert(raised, everyone, hot, moved, scale)
    paired = mine + lax.ppermute(other, "core", swap).astype(F32)
    sent = paired.astype(BF16).reshape(2 * Z * Y, VB // (4 * Z * Y), BLK)
    arrived = lax.all_to_all(sent, ("dom", "px"), 0, 0, tiled=True)
    return (jnp.sum(arrived.astype(F32), axis=0), evidence.reshape(rows))


def solution(mesh):
    split = Mesh(mesh.devices.reshape(2, 2, 2, Z * Y), ("half", "px", "core", "dom"))
    in_specs = (
        P(("half", "dom"), None),
        P(("half", "dom"), None),
        P(("half", "px", "core", "dom"), None),
        P(("half", "px", "core"), None),
    )
    out_specs = (P(("half", "px", "core", "dom"), None), P(("half", "dom")))
    return jax.shard_map(shards, mesh=split, in_specs=in_specs, out_specs=out_specs, check_vma=False)
```

```python
import functools
import math

import jax
import jax.numpy as jnp
import numpy as np
from jax import lax
from jax.experimental import pallas as pl
from jax.experimental.pallas import tpu as pltpu
from jax.sharding import Mesh
from jax.sharding import PartitionSpec as P

PIX = 64
SHIFTS = 9
GRID = 7
OFFS = GRID * GRID
KPAD = 112
CUT = 16
Z, Y = 8, 4
SEG = 8
BLK = 1024
VB = 256
OFFSET_SIGMA = 2.0
BF16 = jnp.bfloat16
F32 = jnp.float32


def dom_of(z, y):
    return (z % Z) * Y + y % Y


FAR = ((0, 0), (2, 2), (4, 0), (-2, 2))
NEAR = ((0, 0), (-1, 0), (0, 1), (0, -1), (1, 0), (-2, 0), (-1, 1), (-1, -1))


def receive_from(dz, dy):
    return [(dom_of(z + dz, y + dy), dom_of(z, y)) for z in range(Z) for y in range(Y)]


def phase_parts():
    offset = np.arange(OFFS)
    a, b = offset // GRID - GRID // 2, offset % GRID - GRID // 2
    f = np.arange(PIX) - PIX // 2
    turns = (f[:, None, None] * a[None, :, None] + f[None, None, :] * b[None, :, None]) % PIX
    angle = -2.0 * math.pi / PIX * turns
    cos, sin = np.cos(angle), np.sin(angle)
    table = np.concatenate([cos, cos, -sin, sin], axis=2).astype(np.float32)
    high = table.astype(BF16)
    low = (table - high.astype(np.float32)).astype(BF16)
    pad = np.zeros((PIX, KPAD - 2 * OFFS, 4 * PIX), BF16)
    return np.concatenate([high, low, pad], axis=1)


def one_hot(index_ref):
    rows = index_ref.shape[1]
    k = lax.broadcasted_iota(jnp.int32, (KPAD, rows), 0)
    offset = jnp.where(k < 2 * OFFS, k % OFFS, -1)
    return jnp.concatenate(
        [jnp.where(offset == index_ref[t : t + 1, :], 1.0, 0.0) for t in range(SHIFTS)], axis=1
    )


def shift_kernel(start, index_ref, image_ref, table_ref, out_ref, hot_ref):
    rows = image_ref.shape[0]
    hot_ref[...] = one_hot(index_ref).T.astype(BF16)
    for u in range(table_ref.shape[0]):
        phase = jnp.dot(hot_ref[...], table_ref[u], preferred_element_type=F32)
        cols = slice(u * 2 * PIX, (u + 1) * 2 * PIX)
        source = slice((start + u) * 2 * PIX, (start + u + 1) * 2 * PIX)
        x = image_ref[:, source].astype(F32)
        swapped = pltpu.roll(x, PIX, 1)
        for t in range(SHIFTS):
            part = phase[t * rows : (t + 1) * rows]
            out_ref[t * rows : (t + 1) * rows, cols] = (
                x * part[:, : 2 * PIX] + swapped * part[:, 2 * PIX :]
            ).astype(BF16)


VMEM = pl.BlockSpec(memory_space=pltpu.VMEM)


def params():
    return pltpu.CompilerParams(vmem_limit_bytes=24 << 20)


def shift_images(images, index_t, table, start):
    total = images.shape[0] * SHIFTS
    count = table.shape[0]
    return pl.pallas_call(
        functools.partial(shift_kernel, start),
        in_specs=[VMEM] * 3,
        out_specs=VMEM,
        out_shape=jax.ShapeDtypeStruct((total, count * 2 * PIX), BF16),
        scratch_shapes=[pltpu.VMEM((total, KPAD), BF16)],
        compiler_params=params(),
        cost_estimate=pl.CostEstimate(flops=count * 10**8, bytes_accessed=count << 18, transcendentals=0),
        name="shift",
    )(index_t, images, jnp.asarray(table))


def choose(g, values):
    out = jnp.zeros_like(g)
    for i, v in enumerate(values):
        if v:
            out = jnp.where(g == i, v, out)
    return out


def slots_kernel(slot_ref, hot_ref):
    count = slot_ref.shape[1]
    dom = lax.axis_index("dom")
    q = lax.broadcasted_iota(jnp.int32, (count, count), 1)
    piece, j = q // 16, (q // 4) % 4
    z = (dom // Y + choose(piece, [d for d, _ in NEAR]) + choose(j, [d for d, _ in FAR]) + Z) % Z
    y = (dom % Y + choose(piece, [d for _, d in NEAR]) + choose(j, [d for _, d in FAR]) + Y) % Y
    source = (z * Y + y) * 4 + q % 4
    order = jnp.where(lax.broadcasted_iota(jnp.int32, (count, count), 0) == source, 1.0, 0.0)
    slots = jnp.dot(
        slot_ref[...].astype(F32).astype(BF16), order.astype(BF16), preferred_element_type=F32
    ).astype(jnp.int32)
    core = lax.axis_index("core")
    m = lax.broadcasted_iota(jnp.int32, (VB, count), 0)
    half = m % (VB // 2)
    owner = jnp.where(m < VB // 2, core, 1 - core)
    block = (half // 2) % 2 * (VB // 2) + owner * (VB // 4) + half // 4 * 2 + half % 2
    for s in range(SEG):
        hot_ref[s] = jnp.where(block == slots[s : s + 1, :], 1.0, 0.0).astype(BF16)


def place_slots(slots_t):
    return pl.pallas_call(
        slots_kernel,
        in_specs=[VMEM],
        out_specs=VMEM,
        out_shape=jax.ShapeDtypeStruct((SEG, VB, slots_t.shape[1]), BF16),
        compiler_params=params(),
        cost_estimate=pl.CostEstimate(flops=10**8, bytes_accessed=4 << 20, transcendentals=0),
        name="slots",
    )(slots_t)


def tile_shifts(x):
    return jnp.concatenate([x] * SHIFTS, axis=1)


def over_shifts(op, x, rows):
    return functools.reduce(op, [x[:, t * rows : (t + 1) * rows] for t in range(SHIFTS)])


def score_kernel(n_moved, *refs):
    index_ref, raised, stats, acc = refs[-4:]
    moved, pieces = refs[:n_moved], refs[n_moved:-4]
    total, count = acc.shape
    norm = jnp.zeros((count, 1), F32)
    start = 0
    for m in moved:
        for c in range(m.shape[1] // BLK):
            at = slice(start + c * BLK, start + (c + 1) * BLK)
            some = jnp.concatenate([p[:, at] for p in pieces], axis=0)
            part = lax.dot_general(
                m[:, c * BLK : (c + 1) * BLK], some, (((1,), (1,)), ((), ())), preferred_element_type=F32
            )
            acc[...] = acc[...] + part if at.start else part
            wide = some.astype(F32)
            norm += jnp.sum(wide * wide, axis=1, keepdims=True)
        start += m.shape[1]
    k = lax.broadcasted_iota(jnp.int32, (8, KPAD), 1)
    a, b = k // GRID - GRID // 2, k % GRID - GRID // 2
    cost = (a * a + b * b).astype(F32) * (0.5 / (OFFSET_SIGMA * OFFSET_SIGMA))
    pen = jnp.dot(
        jnp.where(k < OFFS, cost, 0.0).astype(BF16), one_hot(index_ref).astype(BF16), preferred_element_type=F32
    )
    rows = total // SHIFTS
    scores = acc[...].T - 0.5 * norm - pen[0:1, :]
    top = over_shifts(jnp.maximum, jnp.max(scores, axis=0, keepdims=True), rows)
    value = jnp.exp(scores - tile_shifts(top))
    raised[...] = value
    stats[0:1, :] = top
    stats[1:2, :] = over_shifts(jnp.add, jnp.sum(value, axis=0, keepdims=True), rows)


def score(pieces, moved, index_t):
    total = moved[0].shape[0]
    count = sum(p.shape[0] for p in pieces)
    return pl.pallas_call(
        functools.partial(score_kernel, len(moved)),
        in_specs=[VMEM] * (len(pieces) + len(moved) + 1),
        out_specs=[VMEM, VMEM],
        out_shape=[
            jax.ShapeDtypeStruct((count, total), F32),
            jax.ShapeDtypeStruct((2, total // SHIFTS), F32),
        ],
        scratch_shapes=[pltpu.VMEM((total, count), F32)],
        compiler_params=params(),
        cost_estimate=pl.CostEstimate(flops=2 * 10**9, bytes_accessed=12 << 20, transcendentals=1 << 17),
        name="score",
    )(*moved, *pieces, index_t)


def insert_kernel(scale, raised, s0, s1, s2, s3, hot, *rest):
    moved, (mine, other, evidence, weight) = rest[:-4], rest[-4:]
    tops = [s[0:1, :] for s in (s0, s1, s2, s3)]
    sums = [s[1:2, :] for s in (s0, s1, s2, s3)]
    top = functools.reduce(jnp.maximum, tops)
    total = functools.reduce(jnp.add, [b * jnp.exp(a - top) for a, b in zip(tops, sums)])
    evidence[...] = top + jnp.log(total)
    factor = jnp.exp(tops[0] - top) / total
    weight[...] = (raised[...] * tile_shifts(factor)).astype(BF16)
    blocked = [jnp.dot(hot[s], weight[...], preferred_element_type=F32).astype(BF16) for s in range(SEG)]
    parts = [m[:, s : s + BLK] for m in moved for s in range(0, m.shape[1], BLK)]
    acc = jnp.dot(
        jnp.concatenate(blocked, axis=1), jnp.concatenate(parts, axis=0), preferred_element_type=F32
    )
    mine[...] = acc[: VB // 2] * scale
    other[...] = (acc[VB // 2 :] * scale).astype(BF16)


def insert(raised, stats, hot, moved, scale):
    count, total = raised.shape
    rows = total // SHIFTS
    return pl.pallas_call(
        functools.partial(insert_kernel, scale),
        in_specs=[VMEM] * (2 + len(stats) + len(moved)),
        out_specs=[VMEM] * 3,
        out_shape=[
            jax.ShapeDtypeStruct((VB // 2, BLK), F32),
            jax.ShapeDtypeStruct((VB // 2, BLK), BF16),
            jax.ShapeDtypeStruct((1, rows), F32),
        ],
        scratch_shapes=[pltpu.VMEM((count, total), BF16)],
        compiler_params=params(),
        cost_estimate=pl.CostEstimate(flops=3 * 10**9, bytes_accessed=12 << 20, transcendentals=0),
        name="insert",
    )(raised, *stats, hot, *moved)


def gather(references, early, late):
    far = [lax.ppermute(references, "dom", receive_from(*d)) for d in FAR[1:]]
    far, early = lax.optimization_barrier((far, early()))
    own = jnp.concatenate([references, *far], axis=0)
    first = [lax.ppermute(own, "dom", receive_from(*d)) for d in NEAR[1:5]]
    up = first[0]
    second = [lax.ppermute(up, "dom", receive_from(*d)) for d in ((-1, 0), (0, 1), (0, -1))]
    return [own, *first, *second], (early, late())


def shards(images, shift_index, references, slot_blocks):
    rows = images.shape[0]
    scale = (rows * Z * Y * SEG / VB) ** (-0.5)
    index_t, table = shift_index.T, phase_parts()
    pieces, moved = gather(
        references,
        lambda: shift_images(images, index_t, table[:CUT], 0),
        lambda: shift_images(images, index_t, table[CUT:], CUT),
    )
    hot = place_slots(slot_blocks.T)
    raised, stats = score(pieces, moved, index_t)
    swap = [(0, 1), (1, 0)]
    everyone = [
        stats,
        lax.ppermute(stats, ("px", "core"), [(i, 3 - i) for i in range(4)]),
        lax.ppermute(stats, "px", swap),
        lax.ppermute(stats, "core", swap),
    ]
    mine, other, evidence = insert(raised, everyone, hot, moved, scale)
    paired = mine + lax.ppermute(other, "core", swap).astype(F32)
    sent = paired.astype(BF16).reshape(2 * Z * Y, VB // (4 * Z * Y), BLK)
    arrived = lax.all_to_all(sent, ("dom", "px"), 0, 0, tiled=True)
    return (jnp.sum(arrived.astype(F32), axis=0), evidence.reshape(rows))


def solution(mesh):
    split = Mesh(mesh.devices.reshape(2, 2, 2, Z * Y), ("half", "px", "core", "dom"))
    in_specs = (
        P(("half", "dom"), None),
        P(("half", "dom"), None),
        P(("half", "px", "core", "dom"), None),
        P(("half", "px", "core"), None),
    )
    out_specs = (P(("half", "px", "core", "dom"), None), P(("half", "dom")))
    return jax.shard_map(shards, mesh=split, in_specs=in_specs, out_specs=out_specs, check_vma=False)
```
